1024 devices in a mesh: grp: 16 (over y, z_hi), ep: 64 (over x, z_lo, core).
Axes of the slice: x: 4, y: 8, z: 16 (z_hi: 2, z_lo: 8; z = z_hi * 8 + z_lo), core: 2. Of those that a mesh axis runs over, the one named last changes fastest.
Arguments:
- tokens: bfloat16 [4096, 7168], P('ep', 'grp'), may hold values from -6 to 6
- expert_ids: int32 [4096, 2], P('ep'), may hold values from 0 to 15, all different within a row; in each aligned block of 64 rows (0 to 63, 64 to 127, ...) at most 16 rows name the same one
- route_weight: float32 [4096, 2], P('ep'), may hold values from 0.1 to 1
- out_grad: bfloat16 [4096, 7168], P('ep', 'grp'), may hold values from -6 to 6
- w_gate: bfloat16 [64, 7168, 256], P('ep', 'grp'), may hold values from -0.0625 to 0.0625
- w_up: bfloat16 [64, 7168, 256], P('ep', 'grp'), may hold values from -0.0625 to 0.0625
- w_down: bfloat16 [64, 256, 7168], P('ep', None, 'grp'), may hold values from -0.1875 to 0.1875
Outputs:
- mixed: float32 [4096, 7168], P('ep', 'grp')
- tokens_grad: float32 [4096, 7168], P('ep', 'grp')
- gate_grad: float32 [64, 7168, 256], P('ep', 'grp')
- up_grad: float32 [64, 7168, 256], P('ep', 'grp')
- down_grad: float32 [64, 256, 7168], P('ep', None, 'grp')
The draws below stay inside these ranges and needn't reach their ends.
Inputs may be any that keep to these rules, and one draw needn't show every extreme that they name: `expert_ids`: each token names 2 different experts. Among the 64 tokens of one index of ep no expert is named by more than 16 tokens, a bound that some block reaches.
All inputs are finite; a program needn't handle non-finite values.
Results may differ from the reference program's by a relative error of at most 0.007.
Values may be sent and summed in bfloat16 or wider, within the bound.
No kernel may reach another device: no remote copies, remote signals or barrier semaphores. Data moves between devices by JAX's collectives and lax.ppermute only.
A program may use at most 32 MiB of HBM per device.

```python
import math
import jax
import jax.numpy as jnp
import numpy as np
from jax import lax

D = 7168
HID = 1024
SLICES = 4
TOP = 2
TOK_DEV = 64
HS = 256
EXPERTS = 16
TOKENS = 4096
CAP = 16
N_EP = 64


def steps_of(key, shape, shards, least, largest):
    def one(dim, blocks):
        heights = jax.random.uniform(jax.random.fold_in(jax.random.fold_in(key, 6), dim), (blocks,), jnp.float32, least / len(shards), largest / len(shards))
        return jnp.repeat(jnp.exp(heights), shape[dim] // blocks).reshape((-1,) + (1,) * (len(shape) - dim - 1))

    level = one(*shards[0])
    for cut in shards[1:]:
        level = level * one(*cut)
    return level


def assign_block(key, own, number, rows, number_of, top, most, skew):
    ranking = jax.random.permutation(key, number_of)
    crowded, common = shares(number_of, rows * top, most, skew, True), shares(number_of, rows * top, most, skew, False)
    places = jnp.arange(number_of)

    def named(lengths, turn):
        used = int((lengths > 0).sum())
        fixed = max(1, used // 4)
        moved = fixed + (places - fixed + turn * (used - fixed)) % max(1, number_of - fixed)
        return jnp.zeros((number_of,), jnp.int32).at[ranking[jnp.where(places < fixed, places, moved)]].set(jnp.asarray(lengths, jnp.int32))

    lengths = jnp.where(number % 4 == 0, named(crowded, number // 4), named(common, number - number // 4 - 1))
    mixed = jax.random.permutation(jax.random.fold_in(own, 3), number_of)
    giver, taker = mixed[0:number_of // 2 * 2:2], mixed[1:number_of // 2 * 2:2]
    room = jnp.minimum(lengths[giver] - 1, most - lengths[taker]) // 2
    room = jnp.where((giver == ranking[0]) | (taker == ranking[0]) | (lengths[taker] == 0), 0, jnp.maximum(room, 0))
    moved = jax.random.randint(jax.random.fold_in(own, 4), (number_of // 2,), 0, 1 << 20) % (room + 1)
    lengths = lengths.at[giver].add(-moved).at[taker].add(moved)
    labels = jnp.searchsorted(jnp.cumsum(lengths), jnp.arange(rows * top), side="right").astype(jnp.int32)
    grid = labels.reshape(top, rows).T
    grid = grid[jax.random.permutation(jax.random.fold_in(own, 1), rows)]
    turn = jax.random.randint(jax.random.fold_in(own, 2), (rows, 1), 0, top)
    return jnp.take_along_axis(grid, (jnp.arange(top)[None, :] + turn) % top, axis=1)


def shares(count, total, bound, skew, full):
    portions = [(1 << 20) // math.isqrt(standing ** skew) + 1 for standing in range(1, count + 1)]
    largest = bound if full else min(bound, max(-(-total // count), total * portions[0] // sum(portions)))
    least = 1 if total - largest >= count - 1 else 0
    given, spare = [largest] + [least] * (count - 1), total - largest - least * (count - 1)
    while spare > 0:
        candidates = [i for i in range(1, count) if given[i] < largest] or [i for i in range(1, count) if given[i] < bound]
        mass, left = sum([portions[i] for i in candidates]), spare
        for i in candidates:
            more = min(bound - given[i], max(1, left * portions[i] // mass), spare)
            given[i] = given[i] + more
            spare = spare - more
    return np.array(given)


def normal_values(key, extent, spread, bound, cuts=(), kind=jnp.bfloat16):
    result = spread * jax.random.normal(key, extent, jnp.float32)
    if cuts:
        result = result * steps_of(key, extent, cuts, -0.22, 0.18)
    return jnp.clip(result, -bound, bound).astype(kind)


def setup_inputs(seed: int = 0) -> dict:
    arg_keys = jax.random.split(jax.random.key(seed), 8)
    tokens = normal_values(arg_keys[0], (TOKENS, D), 1.0, 6.0, ((0, 64), (1, 16)))
    expert_ids_keys = jax.random.split(jax.random.fold_in(arg_keys[1], 1), TOKENS // TOK_DEV)
    expert_ids_turns = jax.random.permutation(jax.random.fold_in(arg_keys[1], 3), TOKENS // TOK_DEV)
    expert_ids = jax.vmap(lambda own, number: assign_block(jax.random.fold_in(arg_keys[1], 2), own, number, TOK_DEV, EXPERTS, TOP, CAP, 2))(expert_ids_keys, expert_ids_turns).reshape((TOKENS, TOP))
    route_weight = jnp.clip(0.1 + 0.9 * jax.random.uniform(arg_keys[2], (TOKENS, TOP), jnp.float32) ** steps_of(arg_keys[2], (TOKENS, TOP), ((0, 64),), -0.2, 0.2), 0.1, 1.0)
    out_grad = normal_values(arg_keys[3], (TOKENS, D), 1.0, 6.0, ((0, 64), (1, 16)))
    w_gate = normal_values(arg_keys[4], (N_EP, D, HS), D ** -0.5, 0.0625, ((0, 64), (1, 16)))
    w_up = normal_values(arg_keys[5], (N_EP, D, HS), D ** -0.5, 0.0625, ((0, 64), (1, 16)))
    w_down = normal_values(arg_keys[6], (N_EP, HS, D), HID ** -0.5, 0.1875, ((0, 64), (2, 16)))
    return {"tokens": tokens, "expert_ids": expert_ids, "route_weight": route_weight, "out_grad": out_grad, "w_gate": w_gate, "w_up": w_up, "w_down": w_down}


def reference(tokens, expert_ids, route_weight, out_grad, w_gate, w_up, w_down):
    n_tokens = tokens.shape[0]
    width = tokens.shape[1]
    flat_ids = expert_ids.reshape(-1).astype(jnp.int32)
    assign_count = flat_ids.shape[0]
    flat_weight = jnp.concatenate([route_weight.reshape(-1), jnp.zeros((1,), jnp.float32)])
    token_ext = jnp.concatenate([tokens, jnp.zeros((1, width), tokens.dtype)])
    grad_ext = jnp.concatenate([out_grad, jnp.zeros((1, width), out_grad.dtype)])
    row_bound = N_EP * CAP
    factor = 1.0 / math.sqrt(8 * TOK_DEV)

    def expert_step(carried, expert):
        mixed_acc, grad_acc = carried
        position = jnp.nonzero(flat_ids == expert, size=row_bound, fill_value=assign_count)[0].astype(jnp.int32)
        tok_index = jnp.where(position < assign_count, position // TOP, n_tokens).astype(jnp.int32)
        weight = flat_weight[position]
        expert_rows = token_ext[tok_index]
        grad_rows = (weight[:, None] * grad_ext[tok_index].astype(jnp.float32)).astype(jnp.bfloat16)
        start = (expert * SLICES).astype(jnp.int32)
        gate_slices = lax.dynamic_slice_in_dim(w_gate, start, SLICES, 0)
        up_slices = lax.dynamic_slice_in_dim(w_up, start, SLICES, 0)
        down_slices = lax.dynamic_slice_in_dim(w_down, start, SLICES, 0)
        gate_full = jnp.transpose(gate_slices, (1, 0, 2)).reshape(width, -1)
        up_full = jnp.transpose(up_slices, (1, 0, 2)).reshape(width, -1)
        down_full = down_slices.reshape(-1, width)
        gate_pre = jnp.dot(expert_rows, gate_full, preferred_element_type=jnp.float32)
        up_pre = jnp.dot(expert_rows, up_full, preferred_element_type=jnp.float32)
        gate_sigmoid = jax.nn.sigmoid(gate_pre)
        hidden = (gate_pre * gate_sigmoid * up_pre).astype(jnp.bfloat16)
        hidden_split = hidden.reshape(row_bound, SLICES, -1).astype(jnp.float32)
        part_out = jnp.einsum('bsh,shd->bsd', hidden_split, down_slices.astype(jnp.float32), precision=lax.Precision.HIGHEST).astype(jnp.bfloat16)
        combined = lax.optimization_barrier(jnp.sum(part_out.astype(jnp.float32), axis=1))
        act_grad = jnp.dot(grad_rows, down_full.T, preferred_element_type=jnp.float32)
        gate_delta = (act_grad * up_pre * gate_sigmoid * (1.0 + gate_pre * (1.0 - gate_sigmoid))).astype(jnp.bfloat16)
        up_delta = (act_grad * gate_pre * gate_sigmoid).astype(jnp.bfloat16)
        gate_split = gate_delta.reshape(row_bound, SLICES, -1).astype(jnp.float32)
        up_split = up_delta.reshape(row_bound, SLICES, -1).astype(jnp.float32)
        part_in = (jnp.einsum('bsh,sdh->bsd', gate_split, gate_slices.astype(jnp.float32), precision=lax.Precision.HIGHEST) + jnp.einsum('bsh,sdh->bsd', up_split, up_slices.astype(jnp.float32), precision=lax.Precision.HIGHEST)).astype(jnp.bfloat16)
        back_rows = lax.optimization_barrier(jnp.sum(part_in.astype(jnp.float32), axis=1))
        mixed_acc = mixed_acc.at[tok_index].add(weight[:, None] * combined)
        grad_acc = grad_acc.at[tok_index].add(back_rows)
        gate_grad = jnp.dot(expert_rows.T, gate_delta, preferred_element_type=jnp.float32) * factor
        up_grad = jnp.dot(expert_rows.T, up_delta, preferred_element_type=jnp.float32) * factor
        down_grad = jnp.dot(hidden.T, grad_rows, preferred_element_type=jnp.float32) * factor
        gate_grad = jnp.transpose(gate_grad.reshape(width, SLICES, -1), (1, 0, 2))
        up_grad = jnp.transpose(up_grad.reshape(width, SLICES, -1), (1, 0, 2))
        down_grad = down_grad.reshape(SLICES, -1, width)
        return ((mixed_acc, grad_acc), (gate_grad, up_grad, down_grad))
    start_acc = (jnp.zeros((n_tokens + 1, width), jnp.float32), jnp.zeros((n_tokens + 1, width), jnp.float32))
    finals, grads = lax.scan(expert_step, start_acc, jnp.arange(EXPERTS, dtype=jnp.int32))
    mixed = finals[0][:n_tokens]
    tokens_grad = finals[1][:n_tokens]
    gate_grad = grads[0].reshape(N_EP, width, -1)
    up_grad = grads[1].reshape(N_EP, width, -1)
    down_grad = grads[2].reshape(N_EP, -1, width)
    return (mixed, tokens_grad, gate_grad, up_grad, down_grad)
```

```python
import math

import jax
import jax.numpy as jnp
from jax import lax
from jax.sharding import Mesh, PartitionSpec as P

TOP = 2
CAP = 16
EXPERTS = 16
OWN = ("x", "zp")
SLICE = ("zb", "c")
EP = OWN + SLICE
GRP = ("y", "zh")

LAST = (((1,), (1,)), ((), ()))
FIRST = (((0,), (0,)), ((), ()))
F32 = jnp.float32
BF = jnp.bfloat16


def dot(a, b, dims=(((1,), (0,)), ((), ()))):
    return lax.dot_general(a, b, dims, preferred_element_type=F32)


def swap(value, axis):
    return lax.all_to_all(value, axis, split_axis=0, concat_axis=0, tiled=True)


def sum_y(part):
    rows, cols = part.shape
    got = swap(part.astype(BF).reshape(8, rows // 8, cols), "y")
    return jnp.sum(got.astype(F32), axis=0)


def sum_zh(part):
    other = lax.ppermute(part.astype(BF), "zh", [(0, 1), (1, 0)])
    return part + other.astype(F32)


def body(tokens, expert_ids, route_weight, out_grad, w_gate, w_up, w_down):
    tok_rows, width = tokens.shape
    slots = EXPERTS * CAP
    ids = expert_ids.reshape(-1)
    weight = route_weight.reshape(-1)
    owner_mask = ids[:, None] == jnp.arange(EXPERTS, dtype=jnp.int32)[None, :]
    running = jnp.cumsum(owner_mask.astype(jnp.int32), axis=0)
    target = ids * CAP + jnp.sum(jnp.where(owner_mask, running - 1, 0), axis=1)
    hit = jnp.arange(slots, dtype=jnp.int32)[:, None] == target[None, :]
    slot_weight = jnp.sum(jnp.where(hit, weight[None, :], 0.0), axis=1)
    pick = jnp.sum(hit.reshape(slots, tok_rows, TOP).astype(F32), axis=2).astype(BF)
    place = hit.astype(BF)

    send_tokens = dot(pick, tokens).astype(BF)
    send_grads = (slot_weight[:, None] * dot(pick, out_grad)).astype(BF)

    def dispatch(value):
        got = swap(value.reshape(EXPERTS, CAP, width), OWN)
        return lax.all_gather(got.reshape(slots, width), SLICE, axis=0, tiled=True)

    rows = dispatch(send_tokens)
    grad_rows = dispatch(send_grads)
    w_gate, w_up, w_down = w_gate[0], w_up[0], w_down[0]
    w_in = jnp.concatenate([w_gate, w_up], axis=1)
    hs = w_gate.shape[1]

    pre = sum_zh(sum_y(dot(rows, w_in)))
    act_grad = sum_zh(sum_y(dot(grad_rows, w_down, LAST)))
    gate_pre, up_pre = pre[:, :hs], pre[:, hs:]
    sig = jax.nn.sigmoid(gate_pre)
    hidden = (gate_pre * sig * up_pre).astype(BF)
    gate_delta = (act_grad * up_pre * sig * (1.0 + gate_pre * (1.0 - sig))).astype(BF)
    up_delta = (act_grad * gate_pre * sig).astype(BF)
    deltas = jnp.concatenate([gate_delta, up_delta], axis=1)

    hidden = swap(jnp.broadcast_to(hidden[None], (8,) + hidden.shape), "y").reshape(-1, hs)
    deltas = lax.all_gather(deltas, "y", axis=0, tiled=True)

    def collect(value):
        got = swap(value.astype(BF).reshape(4, slots, width), SLICE)
        summed = jnp.sum(got.astype(F32), axis=0).astype(BF)
        return swap(summed.reshape(EXPERTS, CAP, width), OWN).reshape(slots, width)

    back_out = collect(dot(hidden, w_down))
    back_in = collect(dot(deltas, w_in, LAST))

    factor = 1.0 / math.sqrt(8 * tok_rows)
    gate_grad = (dot(rows, deltas[:, :hs], FIRST) * factor)[None]
    up_grad = (dot(rows, deltas[:, hs:], FIRST) * factor)[None]
    down_grad = (dot(hidden, grad_rows, FIRST) * factor)[None]

    per_out = dot(place, back_out, FIRST) * weight[:, None]
    mixed = jnp.sum(per_out.reshape(tok_rows, TOP, width), axis=1)
    tokens_grad = dot(pick, back_in, FIRST)
    return (mixed, tokens_grad, gate_grad, up_grad, down_grad)


def solution(mesh):
    fine = Mesh(mesh.devices.reshape(8, 2, 4, 4, 2, 2), GRP + EP)
    return jax.shard_map(
        body,
        mesh=fine,
        in_specs=(
            P(EP, GRP),
            P(EP, None),
            P(EP, None),
            P(EP, GRP),
            P(EP, GRP, None),
            P(EP, GRP, None),
            P(EP, None, GRP),
        ),
        out_specs=(
            P(EP, GRP),
            P(EP, GRP),
            P(EP, GRP, None),
            P(EP, GRP, None),
            P(EP, None, GRP),
        ),
        check_vma=False,
    )
```

```python
import math

import jax
import jax.numpy as jnp
from jax import lax
from jax.sharding import Mesh, PartitionSpec as P

TOP = 2
CAP = 16
EXPERTS = 16
OWN = ("x", "zp")
SLICE = ("zb", "c")
EP = OWN + SLICE
GRP = ("y", "zh")

LAST = (((1,), (1,)), ((), ()))
FIRST = (((0,), (0,)), ((), ()))
F32 = jnp.float32
BF = jnp.bfloat16


def dot(a, b, dims=(((1,), (0,)), ((), ()))):
    return lax.dot_general(a, b, dims, preferred_element_type=F32)


def swap(value, axis):
    return lax.all_to_all(value, axis, split_axis=0, concat_axis=0, tiled=True)


def sum_y(part):
    rows, cols = part.shape
    got = swap(part.astype(BF).reshape(8, rows // 8, cols), "y")
    return jnp.sum(got.astype(F32), axis=0)


def sum_zh(part):
    other = lax.ppermute(part.astype(BF), "zh", [(0, 1), (1, 0)])
    return part + other.astype(F32)


def gather_y(part):
    rows, cols = part.shape
    return swap(jnp.broadcast_to(part[None], (8, rows, cols)), "y").reshape(8 * rows, cols)


def body(tokens, expert_ids, route_weight, out_grad, w_gate, w_up, w_down):
    tok_rows, width = tokens.shape
    slots = EXPERTS * CAP
    ids = expert_ids.reshape(-1)
    weight = route_weight.reshape(-1)
    owner_mask = ids[:, None] == jnp.arange(EXPERTS, dtype=jnp.int32)[None, :]
    running = jnp.cumsum(owner_mask.astype(jnp.int32), axis=0)
    target = ids * CAP + jnp.sum(jnp.where(owner_mask, running - 1, 0), axis=1)
    hit = jnp.arange(slots, dtype=jnp.int32)[:, None] == target[None, :]
    slot_weight = jnp.sum(jnp.where(hit, weight[None, :], 0.0), axis=1)
    pick = jnp.sum(hit.reshape(slots, tok_rows, TOP).astype(F32), axis=2).astype(BF)
    place = hit.astype(BF)

    send_tokens = dot(pick, tokens).astype(BF)
    send_grads = (slot_weight[:, None] * dot(pick, out_grad)).astype(BF)

    def dispatch(value):
        got = swap(value.reshape(EXPERTS, CAP, width), OWN)
        return lax.all_gather(got.reshape(slots, width), SLICE, axis=0, tiled=True)

    rows = dispatch(send_tokens)
    grad_rows = dispatch(send_grads)
    w_gate, w_up, w_down = w_gate[0], w_up[0], w_down[0]
    w_in = jnp.concatenate([w_gate, w_up], axis=1)
    hs = w_gate.shape[1]

    pre_part = sum_y(dot(rows, w_in))
    act_part = sum_y(dot(grad_rows, w_down, LAST))
    pre = sum_zh(pre_part)
    gate_pre, up_pre = pre[:, :hs], pre[:, hs:]
    sig = jax.nn.sigmoid(gate_pre)
    hidden = (gate_pre * sig * up_pre).astype(BF)
    hidden, act_part = lax.optimization_barrier((hidden, act_part))
    hidden = gather_y(hidden)
    act_grad = sum_zh(act_part)
    gate_delta = (act_grad * up_pre * sig * (1.0 + gate_pre * (1.0 - sig))).astype(BF)
    up_delta = (act_grad * gate_pre * sig).astype(BF)
    deltas = gather_y(jnp.concatenate([gate_delta, up_delta], axis=1))

    core = lax.axis_index("c")
    half = lax.axis_index("zb")

    def collect(value, matrix, dims):
        parts = value.reshape(2, 2, slots, value.shape[1])

        def term(index):
            part = lax.dynamic_index_in_dim(parts, index, 1, keepdims=False)
            return dot(part.reshape(2 * slots, -1), matrix, dims)

        got = lax.ppermute(term(1 - core).astype(BF), "c", [(0, 1), (1, 0)])
        both = (term(core) + got.astype(F32)).reshape(2, slots, width)
        away = lax.dynamic_index_in_dim(both, 1 - half, 0, keepdims=False).astype(BF)
        keep = lax.dynamic_index_in_dim(both, half, 0, keepdims=False)
        got = lax.ppermute(away, "zb", [(0, 1), (1, 0)])
        summed = (keep + got.astype(F32)).astype(BF)
        return swap(summed.reshape(EXPERTS, CAP, width), OWN).reshape(slots, width)

    back_out = collect(hidden, w_down, (((1,), (0,)), ((), ())))
    back_in = collect(deltas, w_in, LAST)

    factor = 1.0 / math.sqrt(8 * tok_rows)
    gate_grad = (dot(rows, deltas[:, :hs], FIRST) * factor)[None]
    up_grad = (dot(rows, deltas[:, hs:], FIRST) * factor)[None]
    down_grad = (dot(hidden, grad_rows, FIRST) * factor)[None]

    per_out = dot(place, back_out, FIRST) * weight[:, None]
    mixed = jnp.sum(per_out.reshape(tok_rows, TOP, width), axis=1)
    tokens_grad = dot(pick, back_in, FIRST)
    return (mixed, tokens_grad, gate_grad, up_grad, down_grad)


def solution(mesh):
    fine = Mesh(mesh.devices.reshape(8, 2, 4, 4, 2, 2), GRP + EP)
    return jax.shard_map(
        body,
        mesh=fine,
        in_specs=(
            P(EP, GRP),
            P(EP, None),
            P(EP, None),
            P(EP, GRP),
            P(EP, GRP, None),
            P(EP, GRP, None),
            P(EP, None, GRP),
        ),
        out_specs=(
            P(EP, GRP),
            P(EP, GRP),
            P(EP, GRP, None),
            P(EP, GRP, None),
            P(EP, None, GRP),
        ),
        check_vma=False,
    )
```

```python
import math

import jax
import jax.numpy as jnp
from jax import lax
from jax.experimental import pallas as pl
from jax.experimental.pallas import tpu as pltpu
from jax.sharding import Mesh, PartitionSpec as P

TOP = 2
CAP = 16
EXPERTS = 16
SLICES = 4
OWN = ("x", "zp")
SLICE = ("zb", "c")
EP = OWN + SLICE
GRP = ("y", "zh")

PLAIN = (((1,), (0,)), ((), ()))
LAST = (((1,), (1,)), ((), ()))
FIRST = (((0,), (0,)), ((), ()))
F32 = jnp.float32
BF = jnp.bfloat16


def dot(a, b, dims=PLAIN):
    return lax.dot_general(a, b, dims, preferred_element_type=F32)


def local(kernel, outs, *args):
    size = sum(a.size * a.dtype.itemsize for a in args)
    size += sum(math.prod(shape) * jnp.dtype(kind).itemsize for shape, kind in outs)
    return pl.pallas_call(
        kernel,
        out_shape=[jax.ShapeDtypeStruct(shape, kind) for shape, kind in outs],
        in_specs=[pl.BlockSpec(memory_space=pltpu.VMEM)] * len(args),
        out_specs=[pl.BlockSpec(memory_space=pltpu.VMEM)] * len(outs),
        compiler_params=pltpu.CompilerParams(vmem_limit_bytes=16 * 2**20),
        cost_estimate=pl.CostEstimate(
            flops=2 * 10**9, bytes_accessed=2 * size, transcendentals=0
        ),
    )(*args)


def pack_kernel(ids_ref, weight_ref, tokens_ref, grad_ref, send_ref, place_ref):
    count = ids_ref.shape[1]
    slots = place_ref.shape[0]
    across = jnp.broadcast_to(ids_ref[...], (count, count))
    first = lax.broadcasted_iota(jnp.int32, (count, count), 0)
    second = lax.broadcasted_iota(jnp.int32, (count, count), 1)
    earlier = (across.T == across) & (first < second)
    rank = jnp.sum(jnp.where(earlier, 1.0, 0.0), axis=0, keepdims=True)
    target = ids_ref[...] * CAP + rank.astype(jnp.int32)
    hit = lax.broadcasted_iota(jnp.int32, (slots, count), 0) == target
    slot_weight = jnp.sum(jnp.where(hit, weight_ref[...], 0.0), axis=1, keepdims=True)
    place = jnp.where(hit, 1.0, 0.0).astype(BF)
    place_ref[...] = place
    tokens = tokens_ref[...]
    grads = grad_ref[...]
    rows = dot(place, jnp.concatenate([tokens, tokens], axis=0))
    grad_rows = slot_weight * dot(place, jnp.concatenate([grads, grads], axis=0))
    send_ref[...] = jnp.concatenate([rows, grad_rows], axis=1).astype(BF)


def pre_kernel(rows_ref, gate_ref, up_ref, out_ref):
    slices, width, hs = gate_ref.shape
    rows = rows_ref[:, :width]
    for s in range(slices):
        out_ref[:, s * hs : (s + 1) * hs] = dot(rows, gate_ref[s]).astype(BF)
        t = slices + s
        out_ref[:, t * hs : (t + 1) * hs] = dot(rows, up_ref[s]).astype(BF)


def act_kernel(rows_ref, down_ref, out_ref):
    slices, width, hs = down_ref.shape
    rows = rows_ref[:, width:]
    for s in range(slices):
        out_ref[:, s * hs : (s + 1) * hs] = dot(rows, down_ref[s]).astype(BF)


def back_kernel(hidden_ref, deltas_ref, gate_ref, up_ref, down_ref, out_ref):
    slices, width, hs = gate_ref.shape
    out_rows = in_rows = 0.0
    for s in range(slices):
        here = slice(s * hs, (s + 1) * hs)
        there = slice((slices + s) * hs, (slices + s + 1) * hs)
        out_rows += dot(hidden_ref[:, here], down_ref[s], LAST)
        in_rows += dot(deltas_ref[:, here], gate_ref[s], LAST)
        in_rows += dot(deltas_ref[:, there], up_ref[s], LAST)
    out_ref[...] = jnp.concatenate([out_rows, in_rows], axis=1).astype(BF)


def down_kernel(factor, *refs):
    rows_refs, unit_refs, grad_ref = refs[:SLICES], refs[SLICES:-1], refs[-1]
    width = grad_ref.shape[0]
    total = 0.0
    for rows_ref, unit_ref in zip(rows_refs, unit_refs):
        total += dot(rows_ref[:, width:], unit_ref[...], FIRST)
    grad_ref[...] = total * factor


def in_kernel(factor, *refs):
    rows_refs, unit_refs, grad_refs = refs[:SLICES], refs[SLICES:-2], refs[-2:]
    width, hs = grad_refs[0].shape
    total = 0.0
    for rows_ref, unit_ref in zip(rows_refs, unit_refs):
        total += dot(rows_ref[:, :width], unit_ref[...], FIRST)
    grad_refs[0][...] = total[:, :hs] * factor
    grad_refs[1][...] = total[:, hs:] * factor


def home_kernel(place_ref, weight_ref, back_ref, mixed_ref, grad_ref):
    tok_rows, width = mixed_ref.shape
    count = weight_ref.shape[1]
    weight = jnp.broadcast_to(weight_ref[...], (count, count)).T[:, :1]
    per = dot(place_ref[...], back_ref[...], FIRST)
    per_out = per[:, :width] * weight
    per_in = per[:, width:]
    mixed_ref[...] = per_out[:tok_rows] + per_out[tok_rows:]
    grad_ref[...] = per_in[:tok_rows] + per_in[tok_rows:]


def swap(value, axis):
    return lax.all_to_all(value, axis, split_axis=0, concat_axis=0, tiled=True)


def sum_y(part):
    rows, cols = part.shape
    got = swap(part.reshape(8, rows // 8, cols), "y")
    return jnp.sum(got.astype(F32), axis=0)


def sum_zh(part):
    other = lax.ppermute(part.astype(BF), "zh", [(0, 1), (1, 0)])
    return part + other.astype(F32)


def gather_y(part):
    rows, cols = part.shape
    return swap(jnp.broadcast_to(part[None], (8, rows, cols)), "y").reshape(8 * rows, cols)


def to_slice(value, step):
    return lax.ppermute(value, SLICE, [(i, i ^ step) for i in range(SLICES)])


def body(tokens, expert_ids, route_weight, out_grad, w_gate, w_up, w_down):
    tok_rows, width = tokens.shape
    hs = w_gate.shape[2]
    units = SLICES * hs
    slots = EXPERTS * CAP
    ids = expert_ids.T.reshape(1, -1)
    weight = route_weight.T.reshape(1, -1)
    send, place = local(
        pack_kernel,
        [((slots, 2 * width), BF), ((slots, TOP * tok_rows), BF)],
        ids, weight, tokens, out_grad,
    )
    w_gate, w_up, w_down = w_gate[0], w_up[0], w_down[0].T
    send, w_gate, w_up = lax.optimization_barrier((send, w_gate, w_up))
    rows = swap(send.reshape(EXPERTS, CAP, 2 * width), OWN).reshape(slots, 2 * width)
    all_gate = lax.all_gather(w_gate, SLICE, axis=0)
    all_up = lax.all_gather(w_up, SLICE, axis=0)
    rows, all_gate, all_up, w_down = lax.optimization_barrier((rows, all_gate, all_up, w_down))
    all_down = lax.all_gather(w_down, SLICE, axis=0)

    (pre_local,) = local(pre_kernel, [((slots, 2 * units), BF)], rows, all_gate, all_up)
    pre_part = sum_y(pre_local)
    (act_local,) = local(act_kernel, [((slots, units), BF)], rows, all_down)
    act_local, rows = lax.optimization_barrier((act_local, rows))
    every = [rows] + [to_slice(rows, step) for step in (1, 2, 3)]
    act_part = sum_y(act_local)
    pre = sum_zh(pre_part)
    gate_pre, up_pre = pre[:, :units], pre[:, units:]
    sig = jax.nn.sigmoid(gate_pre)
    hidden = (gate_pre * sig * up_pre).astype(BF)
    hidden, act_part, every = lax.optimization_barrier((hidden, act_part, every))
    hidden = gather_y(hidden)
    act_grad = sum_zh(act_part)
    gate_delta = (act_grad * up_pre * sig * (1.0 + gate_pre * (1.0 - sig))).astype(BF)
    up_delta = (act_grad * gate_pre * sig).astype(BF)
    deltas = gather_y(jnp.concatenate([gate_delta, up_delta], axis=1))

    own = lax.axis_index(SLICE)

    def part(value, step, blocks):
        cut = [
            lax.dynamic_slice_in_dim(value, b * units + (own ^ step) * hs, hs, 1)
            for b in range(blocks)
        ]
        return jnp.concatenate(cut, axis=1)

    def of_slice(value, blocks):
        return [part(value, 0, blocks)] + [
            to_slice(part(value, step, blocks), step) for step in (1, 2, 3)
        ]

    hidden_own = of_slice(hidden, 1)
    deltas, hidden, hidden_own = lax.optimization_barrier((deltas, hidden, hidden_own))
    (back,) = local(
        back_kernel, [((slots, 2 * width), BF)], hidden, deltas, all_gate, all_up, all_down
    )
    back = swap(back.reshape(EXPERTS, CAP, 2 * width), OWN).reshape(slots, 2 * width)

    factor = 1.0 / math.sqrt(8 * tok_rows)

    def down(*refs):
        down_kernel(factor, *refs)

    def into(*refs):
        in_kernel(factor, *refs)

    one = ((width, hs), F32)
    (down_grad,) = local(down, [one], *every, *hidden_own)
    gate_grad, up_grad = local(into, [one, one], *every, *of_slice(deltas, 2))
    mixed, tokens_grad = local(home_kernel, [((tok_rows, width), F32)] * 2, place, weight, back)
    return (mixed, tokens_grad, gate_grad[None], up_grad[None], down_grad.T[None])


def solution(mesh):
    fine = Mesh(mesh.devices.reshape(8, 2, 4, 4, 2, 2), GRP + EP)
    return jax.shard_map(
        body,
        mesh=fine,
        in_specs=(
            P(EP, GRP),
            P(EP, None),
            P(EP, None),
            P(EP, GRP),
            P(EP, GRP, None),
            P(EP, GRP, None),
            P(EP, None, GRP),
        ),
        out_specs=(
            P(EP, GRP),
            P(EP, GRP),
            P(EP, GRP, None),
            P(EP, GRP, None),
            P(EP, None, GRP),
        ),
        check_vma=False,
    )
```

```python
import math

import jax
import jax.numpy as jnp
from jax import lax
from jax.experimental import pallas as pl
from jax.experimental.pallas import tpu as pltpu
from jax.sharding import Mesh, PartitionSpec as P

TOP = 2
CAP = 16
EXPERTS = 16
SLICES = 4
OWN = ("x", "zp")
SLICE = ("zb", "c")
EP = OWN + SLICE
GRP = ("y", "zh")

PLAIN = (((1,), (0,)), ((), ()))
LAST = (((1,), (1,)), ((), ()))
FIRST = (((0,), (0,)), ((), ()))
F32 = jnp.float32
BF = jnp.bfloat16


def dot(a, b, dims=PLAIN):
    return lax.dot_general(a, b, dims, preferred_element_type=F32)


def local(kernel, outs, *args, fetch=0):
    size = sum(a.size * a.dtype.itemsize for a in args)
    size += sum(math.prod(shape) * jnp.dtype(kind).itemsize for shape, kind in outs)
    stay, total = len(args) - fetch, len(args)

    def fetching(*refs):
        results = refs[total : total + len(outs)]
        held, sems = refs[total + len(outs) : -1], refs[-1]
        moves = [
            pltpu.make_async_copy(refs[stay + i], held[i], sems.at[i]) for i in range(fetch)
        ]
        for move in moves:
            move.start()
        for move in moves:
            move.wait()
        kernel(*refs[:stay], *held, *results)

    scratch = [pltpu.VMEM(a.shape, a.dtype) for a in args[stay:]]
    return pl.pallas_call(
        fetching if fetch else kernel,
        out_shape=[jax.ShapeDtypeStruct(shape, kind) for shape, kind in outs],
        in_specs=[pl.BlockSpec(memory_space=pltpu.VMEM)] * stay
        + [pl.BlockSpec(memory_space=pltpu.HBM)] * fetch,
        out_specs=[pl.BlockSpec(memory_space=pltpu.VMEM)] * len(outs),
        scratch_shapes=scratch + [pltpu.SemaphoreType.DMA((fetch,))] if fetch else (),
        compiler_params=pltpu.CompilerParams(vmem_limit_bytes=(56 if fetch else 16) * 2**20),
        cost_estimate=pl.CostEstimate(
            flops=2 * 10**9, bytes_accessed=2 * size, transcendentals=0
        ),
    )(*args)


def pair(ref):
    return jnp.concatenate([ref[0:1], ref[1:2]], axis=1)


def hits(ids_ref):
    ids = pair(ids_ref)
    count = ids.shape[1]
    across = jnp.broadcast_to(ids, (count, count))
    first = lax.broadcasted_iota(jnp.int32, (count, count), 0)
    second = lax.broadcasted_iota(jnp.int32, (count, count), 1)
    earlier = (across.T == across) & (first < second)
    rank = jnp.sum(jnp.where(earlier, 1.0, 0.0), axis=0, keepdims=True)
    target = ids * CAP + rank.astype(jnp.int32)
    return lax.broadcasted_iota(jnp.int32, (EXPERTS * CAP, count), 0) == target


def pack_kernel(ids_ref, weight_ref, tokens_ref, grad_ref, send_ref):
    hit = hits(ids_ref)
    slot_weight = jnp.sum(jnp.where(hit, pair(weight_ref), 0.0), axis=1, keepdims=True)
    place = jnp.where(hit, 1.0, 0.0).astype(BF)
    tokens = tokens_ref[...]
    grads = grad_ref[...]
    rows = dot(place, jnp.concatenate([tokens, tokens], axis=0))
    grad_rows = slot_weight * dot(place, jnp.concatenate([grads, grads], axis=0))
    send_ref[...] = jnp.concatenate([rows, grad_rows], axis=1).astype(BF)


def pre_kernel(rows_ref, *refs):
    out_ref = refs[-1]
    width, hs = refs[0].shape[0], refs[0].shape[1] // 2
    half = out_ref.shape[1] // 2
    rows = rows_ref[:, :width]
    for s in range(SLICES):
        both = dot(rows, refs[s][...]).astype(BF)
        out_ref[:, s * hs : (s + 1) * hs] = both[:, :hs]
        out_ref[:, half + s * hs : half + (s + 1) * hs] = both[:, hs:]


def act_kernel(rows_ref, *refs):
    out_ref = refs[-1]
    width, hs = refs[0].shape
    rows = rows_ref[:, width:]
    for s in range(SLICES):
        out_ref[:, s * hs : (s + 1) * hs] = dot(rows, refs[s][...]).astype(BF)


def sum_kernel(got_ref, sum_ref, round_ref):
    total = jnp.sum(got_ref[...].astype(F32), axis=0)
    sum_ref[...] = total
    round_ref[...] = total.astype(BF)


def hidden_kernel(part_ref, other_ref, hidden_ref):
    units = part_ref.shape[1] // 2
    pre = part_ref[...] + other_ref[...].astype(F32)
    gate_pre, up_pre = pre[:, :units], pre[:, units:]
    hidden = (gate_pre * jax.nn.sigmoid(gate_pre) * up_pre).astype(BF)
    hidden_ref[...] = jnp.broadcast_to(hidden[None], hidden_ref.shape)


def delta_kernel(part_ref, other_ref, act_ref, act_other_ref, delta_ref):
    units = act_ref.shape[1]
    pre = part_ref[...] + other_ref[...].astype(F32)
    act_grad = act_ref[...] + act_other_ref[...].astype(F32)
    gate_pre, up_pre = pre[:, :units], pre[:, units:]
    sig = jax.nn.sigmoid(gate_pre)
    gate_delta = act_grad * up_pre * sig * (1.0 + gate_pre * (1.0 - sig))
    up_delta = act_grad * gate_pre * sig
    shape = (delta_ref.shape[0],) + act_ref.shape
    delta_ref[:, :, :units] = jnp.broadcast_to(gate_delta.astype(BF)[None], shape)
    delta_ref[:, :, units:] = jnp.broadcast_to(up_delta.astype(BF)[None], shape)


def back_kernel(hidden_ref, deltas_ref, *refs):
    out_ref = refs[-1]
    in_refs, down_refs = refs[:SLICES], refs[SLICES:-1]
    hs = down_refs[0].shape[1]
    half = deltas_ref.shape[1] // 2
    out_rows = in_rows = 0.0
    for s in range(SLICES):
        here = slice(s * hs, (s + 1) * hs)
        there = slice(half + s * hs, half + (s + 1) * hs)
        out_rows += dot(hidden_ref[:, here], down_refs[s][...], LAST)
        both = jnp.concatenate([deltas_ref[:, here], deltas_ref[:, there]], axis=1)
        in_rows += dot(both, in_refs[s][...], LAST)
    out_ref[...] = jnp.concatenate([out_rows, in_rows], axis=1).astype(BF)


def down_kernel(factor, *refs):
    rows_refs, unit_refs, grad_ref = refs[:SLICES], refs[SLICES:-1], refs[-1]
    width = grad_ref.shape[0]
    total = 0.0
    for rows_ref, unit_ref in zip(rows_refs, unit_refs):
        total += dot(rows_ref[:, width:], unit_ref[...], FIRST)
    grad_ref[...] = total * factor


def in_kernel(factor, *refs):
    rows_refs, unit_refs, grad_refs = refs[:SLICES], refs[SLICES:-2], refs[-2:]
    width, hs = grad_refs[0].shape
    total = 0.0
    for rows_ref, unit_ref in zip(rows_refs, unit_refs):
        total += dot(rows_ref[:, :width], unit_ref[...], FIRST)
    grad_refs[0][...] = total[:, :hs] * factor
    grad_refs[1][...] = total[:, hs:] * factor


def home_kernel(ids_ref, weight_ref, back_ref, mixed_ref, grad_ref):
    tok_rows, width = mixed_ref.shape
    place = jnp.where(hits(ids_ref), 1.0, 0.0).astype(BF)
    row = pair(weight_ref)
    count = row.shape[1]
    weight = jnp.broadcast_to(row, (count, count)).T[:, :1]
    per = dot(place, back_ref[...], FIRST)
    per_out = per[:, :width] * weight
    per_in = per[:, width:]
    mixed_ref[...] = per_out[:tok_rows] + per_out[tok_rows:]
    grad_ref[...] = per_in[:tok_rows] + per_in[tok_rows:]


def swap(value, axis):
    return lax.all_to_all(value, axis, split_axis=0, concat_axis=0, tiled=True)


def sum_y(part):
    rows, cols = part.shape
    got = swap(part.reshape(8, rows // 8, cols), "y")
    shape = (rows // 8, cols)
    return local(sum_kernel, [(shape, F32), (shape, BF)], got)


def swap_pair(value, axis):
    return lax.ppermute(value, axis, [(0, 1), (1, 0)])


def gather_y(copies):
    count, rows, cols = copies.shape
    return swap(copies, "y").reshape(count * rows, cols)


def to_slice(value, step):
    return lax.ppermute(value, SLICE, [(i, i ^ step) for i in range(SLICES)])


def share(value):
    across = swap_pair(value, "zb")
    return [value, swap_pair(value, "c"), across, swap_pair(across, "c")]


def body(tokens, expert_ids, route_weight, out_grad, w_gate, w_up, w_down):
    tok_rows, width = tokens.shape
    hs = w_gate.shape[2]
    units = SLICES * hs
    slots = EXPERTS * CAP
    ids, weight = expert_ids.T, route_weight.T
    (send,) = local(
        pack_kernel, [((slots, 2 * width), BF)], ids, weight, tokens, out_grad, fetch=4
    )
    send, w_gate, w_up = lax.optimization_barrier((send, w_gate, w_up))
    rows = swap(send.reshape(EXPERTS, CAP, 2 * width), OWN).reshape(slots, 2 * width)
    w_in = share(jnp.concatenate([w_gate[0], w_up[0]], axis=1))
    (pre_local,) = local(pre_kernel, [((slots, 2 * units), BF)], rows, *w_in)
    pre_local, rows, w_down = lax.optimization_barrier((pre_local, rows, w_down))
    pre_part, pre_round = sum_y(pre_local)
    w_out = share(w_down[0].T)
    every = share(rows)
    (act_local,) = local(act_kernel, [((slots, units), BF)], rows, *w_out)
    act_local, every = lax.optimization_barrier((act_local, every))
    act_part, act_round = sum_y(act_local)

    pre_other = swap_pair(pre_round, "zh")
    copies = (8, slots // 8)
    (hidden,) = local(hidden_kernel, [(copies + (units,), BF)], pre_part, pre_other)
    hidden, act_round = lax.optimization_barrier((hidden, act_round))
    hidden = gather_y(hidden)
    act_other = swap_pair(act_round, "zh")
    (deltas,) = local(
        delta_kernel, [(copies + (2 * units,), BF)], pre_part, pre_other, act_part, act_other
    )
    deltas = gather_y(deltas)

    def of_slice(value, blocks):
        cut = [
            [value[:, (b * SLICES + s) * hs :][:, :hs] for b in range(blocks)]
            for s in range(SLICES)
        ]
        cut = [jnp.concatenate(part, axis=1) for part in cut]
        return cut[:1] + [to_slice(cut[step], step) for step in (1, 2, 3)]

    hidden_own = of_slice(hidden, 1)
    deltas, hidden, hidden_own = lax.optimization_barrier((deltas, hidden, hidden_own))
    (back,) = local(
        back_kernel, [((slots, 2 * width), BF)], hidden, deltas, *w_in, *w_out, fetch=10
    )
    back = swap(back.reshape(EXPERTS, CAP, 2 * width), OWN).reshape(slots, 2 * width)

    factor = 1.0 / math.sqrt(8 * tok_rows)

    def down(*refs):
        down_kernel(factor, *refs)

    def into(*refs):
        in_kernel(factor, *refs)

    one = ((width, hs), F32)
    (down_grad,) = local(down, [one], *every, *hidden_own)
    gate_grad, up_grad = local(into, [one, one], *every, *of_slice(deltas, 2))
    mixed, tokens_grad = local(home_kernel, [((tok_rows, width), F32)] * 2, ids, weight, back)
    return (mixed, tokens_grad, gate_grad[None], up_grad[None], down_grad.T[None])


def solution(mesh):
    fine = Mesh(mesh.devices.reshape(8, 2, 4, 4, 2, 2), GRP + EP)
    return jax.shard_map(
        body,
        mesh=fine,
        in_specs=(
            P(EP, GRP),
            P(EP, None),
            P(EP, None),
            P(EP, GRP),
            P(EP, GRP, None),
            P(EP, GRP, None),
            P(EP, None, GRP),
        ),
        out_specs=(
            P(EP, GRP),
            P(EP, GRP),
            P(EP, GRP, None),
            P(EP, GRP, None),
            P(EP, None, GRP),
        ),
        check_vma=False,
    )
```

```python
import math

import jax
import jax.numpy as jnp
from jax import lax
from jax.experimental import pallas as pl
from jax.experimental.pallas import tpu as pltpu
from jax.sharding import Mesh, PartitionSpec as P

TOP = 2
CAP = 16
EXPERTS = 16
SLICES = 4
OWN = ("x", "zp")
SLICE = ("zb", "c")
EP = OWN + SLICE
GRP = ("y", "zh")

PLAIN = (((1,), (0,)), ((), ()))
LAST = (((1,), (1,)), ((), ()))
FIRST = (((0,), (0,)), ((), ()))
F32 = jnp.float32
BF = jnp.bfloat16


def dot(a, b, dims=PLAIN):
    return lax.dot_general(a, b, dims, preferred_element_type=F32)


def local(kernel, outs, *args, fetch=0, scalars=0):
    size = sum(a.size * a.dtype.itemsize for a in args)
    size += sum(math.prod(shape) * jnp.dtype(kind).itemsize for shape, kind in outs)
    stay, total = len(args) - fetch, len(args)

    def fetching(*refs):
        results = refs[total : total + len(outs)]
        held, sems = refs[total + len(outs) : -1], refs[-1]
        moves = [
            pltpu.make_async_copy(refs[stay + i], held[i], sems.at[i]) for i in range(fetch)
        ]
        for move in moves:
            move.start()
        for move in moves:
            move.wait()
        kernel(*refs[:stay], *held, *results)

    scratch = [pltpu.VMEM(a.shape, a.dtype) for a in args[stay:]]
    return pl.pallas_call(
        fetching if fetch else kernel,
        out_shape=[jax.ShapeDtypeStruct(shape, kind) for shape, kind in outs],
        in_specs=[pl.BlockSpec(memory_space=pltpu.SMEM)] * scalars
        + [pl.BlockSpec(memory_space=pltpu.VMEM)] * (stay - scalars)
        + [pl.BlockSpec(memory_space=pltpu.HBM)] * fetch,
        out_specs=[pl.BlockSpec(memory_space=pltpu.VMEM)] * len(outs),
        scratch_shapes=scratch + [pltpu.SemaphoreType.DMA((fetch,))] if fetch else (),
        compiler_params=pltpu.CompilerParams(vmem_limit_bytes=(56 if fetch else 16) * 2**20),
        cost_estimate=pl.CostEstimate(
            flops=2 * 10**9, bytes_accessed=2 * size, transcendentals=0
        ),
    )(*args)


def pair(ref):
    return jnp.concatenate([ref[0:1], ref[1:2]], axis=1)


def hits(ids_ref, owner):
    ids = pair(ids_ref)
    count = ids.shape[1]
    across = jnp.broadcast_to(ids, (count, count))
    first = lax.broadcasted_iota(jnp.int32, (count, count), 0)
    second = lax.broadcasted_iota(jnp.int32, (count, count), 1)
    earlier = (across.T == across) & (first < second)
    rank = jnp.sum(jnp.where(earlier, 1.0, 0.0), axis=0, keepdims=True)
    slot = lax.broadcasted_iota(jnp.int32, (EXPERTS * CAP, count), 0)
    return (owner(slot // CAP) == ids) & (slot % CAP == rank.astype(jnp.int32))


def places(ids_ref, owner):
    return jnp.where(hits(ids_ref, owner), 1.0, 0.0).astype(BF)


def pack_kernel(ids_ref, weight_ref, tokens_ref, grad_ref, send_ref):
    hit = hits(ids_ref, lambda block: block)
    slot_weight = jnp.sum(jnp.where(hit, pair(weight_ref), 0.0), axis=1, keepdims=True)
    place = jnp.where(hit, 1.0, 0.0).astype(BF)
    tokens = tokens_ref[...]
    grads = grad_ref[...]
    rows = dot(place, jnp.concatenate([tokens, tokens], axis=0))
    grad_rows = slot_weight * dot(place, jnp.concatenate([grads, grads], axis=0))
    send_ref[...] = jnp.concatenate([rows, grad_rows], axis=1).astype(BF)


def pre_kernel(rows_ref, *refs):
    out_ref = refs[-1]
    width, hs = refs[0].shape[0], refs[0].shape[1] // 2
    half = out_ref.shape[1] // 2
    rows = rows_ref[:, :width]
    for s in range(SLICES):
        both = dot(rows, refs[s][...]).astype(BF)
        out_ref[:, s * hs : (s + 1) * hs] = both[:, :hs]
        out_ref[:, half + s * hs : half + (s + 1) * hs] = both[:, hs:]


def act_kernel(rows_ref, *refs):
    out_ref = refs[-1]
    width, hs = refs[0].shape
    rows = rows_ref[:, width:]
    for s in range(SLICES):
        out_ref[:, s * hs : (s + 1) * hs] = dot(rows, refs[s][...]).astype(BF)


def sum_kernel(got_ref, sum_ref, round_ref):
    total = jnp.sum(got_ref[...].astype(F32), axis=0)
    sum_ref[...] = total
    round_ref[...] = total.astype(BF)


def hidden_kernel(part_ref, other_ref, hidden_ref):
    units = part_ref.shape[1] // 2
    pre = part_ref[...] + other_ref[...].astype(F32)
    gate_pre, up_pre = pre[:, :units], pre[:, units:]
    hidden = (gate_pre * jax.nn.sigmoid(gate_pre) * up_pre).astype(BF)
    hidden_ref[...] = jnp.broadcast_to(hidden[None], hidden_ref.shape)


def delta_kernel(part_ref, other_ref, act_ref, act_other_ref, delta_ref):
    units = act_ref.shape[1]
    pre = part_ref[...] + other_ref[...].astype(F32)
    act_grad = act_ref[...] + act_other_ref[...].astype(F32)
    gate_pre, up_pre = pre[:, :units], pre[:, units:]
    sig = jax.nn.sigmoid(gate_pre)
    gate_delta = act_grad * up_pre * sig * (1.0 + gate_pre * (1.0 - sig))
    up_delta = act_grad * gate_pre * sig
    shape = (delta_ref.shape[0],) + act_ref.shape
    delta_ref[:, :, :units] = jnp.broadcast_to(gate_delta.astype(BF)[None], shape)
    delta_ref[:, :, units:] = jnp.broadcast_to(up_delta.astype(BF)[None], shape)


def out_kernel(here_ref, hidden_ref, *refs):
    out_ref = refs[-1]
    hs = refs[0].shape[1]
    rows = 0.0
    for s in range(SLICES):
        rows += dot(hidden_ref[:, s * hs : (s + 1) * hs], refs[s][...], LAST)
    rows = rows.astype(BF)
    for e in range(EXPERTS):
        block = ((e // 4) ^ here_ref[0]) * 4 + ((e % 4) ^ here_ref[1])
        to = pl.multiple_of(block * CAP, CAP)
        out_ref[pl.ds(to, CAP), :] = rows[e * CAP : (e + 1) * CAP]


def back_kernel(deltas_ref, *refs):
    out_ref = refs[-1]
    hs = refs[0].shape[1] // 2
    half = deltas_ref.shape[1] // 2
    in_rows = 0.0
    for s in range(SLICES):
        here = slice(s * hs, (s + 1) * hs)
        there = slice(half + s * hs, half + (s + 1) * hs)
        both = jnp.concatenate([deltas_ref[:, here], deltas_ref[:, there]], axis=1)
        in_rows += dot(both, refs[s][...], LAST)
    out_ref[...] = in_rows.astype(BF)


def down_kernel(factor, *refs):
    rows_refs, unit_refs, grad_ref = refs[:SLICES], refs[SLICES:-1], refs[-1]
    width = grad_ref.shape[0]
    total = 0.0
    for rows_ref, unit_ref in zip(rows_refs, unit_refs):
        total += dot(rows_ref[:, width:], unit_ref[...], FIRST)
    grad_ref[...] = total * factor


def in_kernel(factor, *refs):
    rows_refs, unit_refs, grad_refs = refs[:SLICES], refs[SLICES:-2], refs[-2:]
    width, hs = grad_refs[0].shape
    total = 0.0
    for rows_ref, unit_ref in zip(rows_refs, unit_refs):
        total += dot(rows_ref[:, :width], unit_ref[...], FIRST)
    grad_refs[0][...] = total[:, :hs] * factor
    grad_refs[1][...] = total[:, hs:] * factor


def mixed_kernel(here_ref, ids_ref, weight_ref, *refs):
    back_refs, mixed_ref = refs[:-1], refs[-1]
    tok_rows = mixed_ref.shape[0]

    def owner(block):
        return ((block % 4) ^ here_ref[0]) * 4 + ((block // 4) ^ here_ref[1])

    row = pair(weight_ref)
    count = row.shape[1]
    weight = jnp.broadcast_to(row, (count, count)).T[:, :1]
    back = jnp.concatenate([ref[...] for ref in back_refs], axis=0)
    per = dot(places(ids_ref, owner), back, FIRST) * weight
    mixed_ref[...] = per[:tok_rows] + per[tok_rows:]


def grad_kernel(ids_ref, back_ref, grad_ref):
    tok_rows = grad_ref.shape[0]
    per = dot(places(ids_ref, lambda block: block), back_ref[...], FIRST)
    grad_ref[...] = per[:tok_rows] + per[tok_rows:]


def swap(value, axis):
    return lax.all_to_all(value, axis, split_axis=0, concat_axis=0, tiled=True)


def sum_y(part):
    rows, cols = part.shape
    got = swap(part.reshape(8, rows // 8, cols), "y")
    shape = (rows // 8, cols)
    return local(sum_kernel, [(shape, F32), (shape, BF)], got)


def swap_pair(value, axis):
    return lax.ppermute(value, axis, [(0, 1), (1, 0)])


def gather_y(copies):
    count, rows, cols = copies.shape
    return swap(copies, "y").reshape(count * rows, cols)


def step_to(value, axis, step):
    return lax.ppermute(value, axis, [(i, i ^ step) for i in range(4)])


def to_slice(value, step):
    return lax.ppermute(value, SLICE, [(i, i ^ step) for i in range(SLICES)])


def share(value):
    across = swap_pair(value, "zb")
    return [value, swap_pair(value, "c"), across, swap_pair(across, "c")]


def body(tokens, expert_ids, route_weight, out_grad, w_gate, w_up, w_down):
    tok_rows, width = tokens.shape
    hs = w_gate.shape[2]
    units = SLICES * hs
    slots = EXPERTS * CAP
    ids, weight = expert_ids.T, route_weight.T
    (send,) = local(
        pack_kernel, [((slots, 2 * width), BF)], ids, weight, tokens, out_grad, fetch=4
    )
    send, w_gate, w_up = lax.optimization_barrier((send, w_gate, w_up))
    rows = swap(send.reshape(EXPERTS, CAP, 2 * width), OWN).reshape(slots, 2 * width)
    w_in = share(jnp.concatenate([w_gate[0], w_up[0]], axis=1))
    (pre_local,) = local(pre_kernel, [((slots, 2 * units), BF)], rows, *w_in)
    pre_local, rows, w_down = lax.optimization_barrier((pre_local, rows, w_down))
    pre_part, pre_round = sum_y(pre_local)
    w_out = share(w_down[0].T)
    every = share(rows)
    (act_local,) = local(act_kernel, [((slots, units), BF)], rows, *w_out)
    act_local, every = lax.optimization_barrier((act_local, every))
    act_part, act_round = sum_y(act_local)

    pre_other = swap_pair(pre_round, "zh")
    copies = (8, slots // 8)
    (hidden,) = local(hidden_kernel, [(copies + (units,), BF)], pre_part, pre_other)
    hidden, act_round = lax.optimization_barrier((hidden, act_round))
    hidden = gather_y(hidden)
    act_other = swap_pair(act_round, "zh")
    (deltas,) = local(
        delta_kernel, [(copies + (2 * units,), BF)], pre_part, pre_other, act_part, act_other
    )
    deltas = gather_y(deltas)

    def of_slice(value, blocks):
        cut = [
            [value[:, (b * SLICES + s) * hs :][:, :hs] for b in range(blocks)]
            for s in range(SLICES)
        ]
        cut = [jnp.concatenate(part, axis=1) for part in cut]
        return cut[:1] + [to_slice(cut[step], step) for step in (1, 2, 3)]

    here = jnp.stack([lax.axis_index("x"), lax.axis_index("zp")]).astype(jnp.int32)
    (out_rows,) = local(
        out_kernel, [((slots, width), BF)], here, hidden, *w_out, fetch=4, scalars=1
    )
    out_rows = out_rows.reshape(4, 4, CAP, width)
    along = [out_rows[0]] + [step_to(out_rows[step], "x", step) for step in (1, 2, 3)]
    along = [jnp.stack([part[step] for part in along]) for step in range(4)]
    hidden_own = of_slice(hidden, 1)
    home = along[:1] + [step_to(along[step], "zp", step) for step in (1, 2, 3)]
    home = [part.reshape(4 * CAP, width) for part in home]
    deltas, home, hidden_own = lax.optimization_barrier((deltas, home, hidden_own))

    (back,) = local(back_kernel, [((slots, width), BF)], deltas, *w_in, fetch=5)
    back, deltas = lax.optimization_barrier((back, deltas))
    back = swap(back.reshape(EXPERTS, CAP, width), OWN).reshape(slots, width)

    factor = 1.0 / math.sqrt(8 * tok_rows)

    def down(*refs):
        down_kernel(factor, *refs)

    def into(*refs):
        in_kernel(factor, *refs)

    one = ((width, hs), F32)
    (down_grad,) = local(down, [one], *every, *hidden_own)
    gate_grad, up_grad = local(into, [one, one], *every, *of_slice(deltas, 2))
    result = [((tok_rows, width), F32)]
    (mixed,) = local(mixed_kernel, result, here, ids, weight, *home, scalars=1)
    (tokens_grad,) = local(grad_kernel, result, ids, back)
    return (mixed, tokens_grad, gate_grad[None], up_grad[None], down_grad.T[None])


def solution(mesh):
    fine = Mesh(mesh.devices.reshape(8, 2, 4, 4, 2, 2), GRP + EP)
    return jax.shard_map(
        body,
        mesh=fine,
        in_specs=(
            P(EP, GRP),
            P(EP, None),
            P(EP, None),
            P(EP, GRP),
            P(EP, GRP, None),
            P(EP, GRP, None),
            P(EP, None, GRP),
        ),
        out_specs=(
            P(EP, GRP),
            P(EP, GRP),
            P(EP, GRP, None),
            P(EP, GRP, None),
            P(EP, None, GRP),
        ),
        check_vma=False,
    )
```

```python
import math

import jax
import jax.numpy as jnp
from jax import lax
from jax.experimental import pallas as pl
from jax.experimental.pallas import tpu as pltpu
from jax.sharding import Mesh, PartitionSpec as P

TOP = 2
CAP = 16
EXPERTS = 16
SLICES = 4
OWN = ("x", "zp")
SLICE = ("zb", "c")
EP = OWN + SLICE
GRP = ("y", "zh")

PLAIN = (((1,), (0,)), ((), ()))
LAST = (((1,), (1,)), ((), ()))
FIRST = (((0,), (0,)), ((), ()))
F32 = jnp.float32
BF = jnp.bfloat16


def dot(a, b, dims=PLAIN):
    return lax.dot_general(a, b, dims, preferred_element_type=F32)


def local(kernel, outs, *args, fetch=0):
    size = sum(a.size * a.dtype.itemsize for a in args)
    size += sum(math.prod(shape) * jnp.dtype(kind).itemsize for shape, kind in outs)
    stay, total = len(args) - fetch, len(args)

    def fetching(*refs):
        results = refs[total : total + len(outs)]
        held, sems = refs[total + len(outs) : -1], refs[-1]
        moves = [
            pltpu.make_async_copy(refs[stay + i], held[i], sems.at[i]) for i in range(fetch)
        ]
        for move in moves:
            move.start()
        for move in moves:
            move.wait()
        kernel(*refs[:stay], *held, *results)

    scratch = [pltpu.VMEM(a.shape, a.dtype) for a in args[stay:]]
    return pl.pallas_call(
        fetching if fetch else kernel,
        out_shape=[jax.ShapeDtypeStruct(shape, kind) for shape, kind in outs],
        in_specs=[pl.BlockSpec(memory_space=pltpu.VMEM)] * stay
        + [pl.BlockSpec(memory_space=pltpu.HBM)] * fetch,
        out_specs=[pl.BlockSpec(memory_space=pltpu.VMEM)] * len(outs),
        scratch_shapes=scratch + [pltpu.SemaphoreType.DMA((fetch,))] if fetch else (),
        compiler_params=pltpu.CompilerParams(vmem_limit_bytes=(56 if fetch else 16) * 2**20),
        cost_estimate=pl.CostEstimate(
            flops=2 * 10**9, bytes_accessed=2 * size, transcendentals=0
        ),
    )(*args)


def pair(ref):
    return jnp.concatenate([ref[0:1], ref[1:2]], axis=1)


def hits(ids_ref):
    ids = pair(ids_ref)
    count = ids.shape[1]
    across = jnp.broadcast_to(ids, (count, count))
    first = lax.broadcasted_iota(jnp.int32, (count, count), 0)
    second = lax.broadcasted_iota(jnp.int32, (count, count), 1)
    earlier = (across.T == across) & (first < second)
    rank = jnp.sum(jnp.where(earlier, 1.0, 0.0), axis=0, keepdims=True)
    target = ids * CAP + rank.astype(jnp.int32)
    return lax.broadcasted_iota(jnp.int32, (EXPERTS * CAP, count), 0) == target


def pack_kernel(ids_ref, weight_ref, tokens_ref, grad_ref, send_ref):
    hit = hits(ids_ref)
    slot_weight = jnp.sum(jnp.where(hit, pair(weight_ref), 0.0), axis=1, keepdims=True)
    place = jnp.where(hit, 1.0, 0.0).astype(BF)
    tokens = tokens_ref[...]
    grads = grad_ref[...]
    rows = dot(place, jnp.concatenate([tokens, tokens], axis=0))
    grad_rows = slot_weight * dot(place, jnp.concatenate([grads, grads], axis=0))
    send_ref[...] = jnp.concatenate([rows, grad_rows], axis=1).astype(BF)


def pre_kernel(rows_ref, *refs):
    out_ref = refs[-1]
    width, hs = refs[0].shape[0], refs[0].shape[1] // 2
    half = out_ref.shape[1] // 2
    rows = rows_ref[:, :width]
    for s in range(SLICES):
        both = dot(rows, refs[s][...]).astype(BF)
        out_ref[:, s * hs : (s + 1) * hs] = both[:, :hs]
        out_ref[:, half + s * hs : half + (s + 1) * hs] = both[:, hs:]


def act_kernel(rows_ref, *refs):
    out_ref = refs[-1]
    width, hs = refs[0].shape
    rows = rows_ref[:, width:]
    for s in range(SLICES):
        out_ref[:, s * hs : (s + 1) * hs] = dot(rows, refs[s][...]).astype(BF)


def sum_kernel(got_ref, sum_ref, round_ref):
    total = jnp.sum(got_ref[...].astype(F32), axis=0)
    sum_ref[...] = total
    round_ref[...] = total.astype(BF)


def hidden_kernel(part_ref, other_ref, hidden_ref):
    units = part_ref.shape[1] // 2
    pre = part_ref[...] + other_ref[...].astype(F32)
    gate_pre, up_pre = pre[:, :units], pre[:, units:]
    hidden = (gate_pre * jax.nn.sigmoid(gate_pre) * up_pre).astype(BF)
    hidden_ref[...] = jnp.broadcast_to(hidden[None], hidden_ref.shape)


def delta_kernel(part_ref, other_ref, act_ref, act_other_ref, delta_ref):
    units = act_ref.shape[1]
    pre = part_ref[...] + other_ref[...].astype(F32)
    act_grad = act_ref[...] + act_other_ref[...].astype(F32)
    gate_pre, up_pre = pre[:, :units], pre[:, units:]
    sig = jax.nn.sigmoid(gate_pre)
    gate_delta = act_grad * up_pre * sig * (1.0 + gate_pre * (1.0 - sig))
    up_delta = act_grad * gate_pre * sig
    shape = (delta_ref.shape[0],) + act_ref.shape
    delta_ref[:, :, :units] = jnp.broadcast_to(gate_delta.astype(BF)[None], shape)
    delta_ref[:, :, units:] = jnp.broadcast_to(up_delta.astype(BF)[None], shape)


def back_kernel(hidden_ref, deltas_ref, *refs):
    out_ref = refs[-1]
    in_refs, down_refs = refs[:SLICES], refs[SLICES:-1]
    hs = down_refs[0].shape[1]
    half = deltas_ref.shape[1] // 2
    out_rows = in_rows = 0.0
    for s in range(SLICES):
        here = slice(s * hs, (s + 1) * hs)
        there = slice(half + s * hs, half + (s + 1) * hs)
        out_rows += dot(hidden_ref[:, here], down_refs[s][...], LAST)
        both = jnp.concatenate([deltas_ref[:, here], deltas_ref[:, there]], axis=1)
        in_rows += dot(both, in_refs[s][...], LAST)
    out_ref[...] = jnp.concatenate([out_rows, in_rows], axis=1).astype(BF)


def down_kernel(rows_ref, next_ref, own_ref, got_ref, keep_ref, away_ref):
    width, hs = keep_ref.shape
    rows, following = rows_ref[:, width:], next_ref[:, width:]
    for step, out_ref in ((0, keep_ref), (2, away_ref)):
        there = slice(step // 2 * hs, (step // 2 + 1) * hs)
        total = dot(rows, own_ref[:, step * hs : (step + 1) * hs], FIRST)
        total += dot(following, got_ref[:, there], FIRST)
        out_ref[...] = total.astype(out_ref.dtype)


def in_kernel(rows_ref, next_ref, own_ref, got_ref, keep_ref, away_ref):
    width, hs = keep_ref.shape[0], keep_ref.shape[1] // 2
    half = own_ref.shape[1] // 2
    rows, following = rows_ref[:, :width], next_ref[:, :width]
    for step, out_ref in ((0, keep_ref), (2, away_ref)):
        for side in (0, 1):
            here = slice(side * half + step * hs, side * half + (step + 1) * hs)
            there = slice((step + side) * hs, (step + side + 1) * hs)
            total = dot(rows, own_ref[:, here], FIRST)
            total += dot(following, got_ref[:, there], FIRST)
            out_ref[:, side * hs : (side + 1) * hs] = total.astype(out_ref.dtype)


def home_kernel(ids_ref, weight_ref, back_ref, mixed_ref, grad_ref):
    tok_rows, width = mixed_ref.shape
    place = jnp.where(hits(ids_ref), 1.0, 0.0).astype(BF)
    row = pair(weight_ref)
    count = row.shape[1]
    weight = jnp.broadcast_to(row, (count, count)).T[:, :1]
    per = dot(place, back_ref[...], FIRST)
    per_out = per[:, :width] * weight
    per_in = per[:, width:]
    mixed_ref[...] = per_out[:tok_rows] + per_out[tok_rows:]
    grad_ref[...] = per_in[:tok_rows] + per_in[tok_rows:]


def swap(value, axis):
    return lax.all_to_all(value, axis, split_axis=0, concat_axis=0, tiled=True)


def sum_y(part):
    rows, cols = part.shape
    got = swap(part.reshape(8, rows // 8, cols), "y")
    shape = (rows // 8, cols)
    return local(sum_kernel, [(shape, F32), (shape, BF)], got)


def swap_pair(value, axis):
    return lax.ppermute(value, axis, [(0, 1), (1, 0)])


def gather_y(copies):
    count, rows, cols = copies.shape
    return swap(copies, "y").reshape(count * rows, cols)


def share(value):
    across = swap_pair(value, "zb")
    return [value, swap_pair(value, "c"), across, swap_pair(across, "c")]


def body(tokens, expert_ids, route_weight, out_grad, w_gate, w_up, w_down):
    tok_rows, width = tokens.shape
    hs = w_gate.shape[2]
    units = SLICES * hs
    slots = EXPERTS * CAP
    ids, weight = expert_ids.T, route_weight.T
    (send,) = local(
        pack_kernel, [((slots, 2 * width), BF)], ids, weight, tokens, out_grad, fetch=4
    )
    send, w_gate, w_up = lax.optimization_barrier((send, w_gate, w_up))
    rows = swap(send.reshape(EXPERTS, CAP, 2 * width), OWN).reshape(slots, 2 * width)
    w_in = share(jnp.concatenate([w_gate[0], w_up[0]], axis=1))
    (pre_local,) = local(pre_kernel, [((slots, 2 * units), BF)], rows, *w_in)
    pre_local, rows, w_down = lax.optimization_barrier((pre_local, rows, w_down))
    pre_part, pre_round = sum_y(pre_local)
    w_out = share(w_down[0].T)
    rows_next = swap_pair(rows, "c")
    (act_local,) = local(act_kernel, [((slots, units), BF)], rows, *w_out)
    act_part, act_round = sum_y(act_local)

    pre_other = swap_pair(pre_round, "zh")
    copies = (8, slots // 8)
    (hidden,) = local(hidden_kernel, [(copies + (units,), BF)], pre_part, pre_other)
    hidden, act_round, rows_next = lax.optimization_barrier((hidden, act_round, rows_next))
    hidden = gather_y(hidden)
    act_other = swap_pair(act_round, "zh")
    (deltas,) = local(
        delta_kernel, [(copies + (2 * units,), BF)], pre_part, pre_other, act_part, act_other
    )
    deltas = gather_y(deltas)

    def to_next(value):
        sides = value.shape[1] // units
        cut = [
            value[:, side * units + step * hs :][:, :hs] for step in (1, 3) for side in range(sides)
        ]
        return swap_pair(jnp.concatenate(cut, axis=1), "c")

    shape = (width, hs)
    down_keep, down_away = local(
        down_kernel, [(shape, F32), (shape, BF)], rows, rows_next, hidden, to_next(hidden)
    )
    down_got = swap_pair(down_away, "zb")
    deltas, hidden, down_got = lax.optimization_barrier((deltas, hidden, down_got))
    deltas_got = to_next(deltas)
    (back,) = local(
        back_kernel, [((slots, 2 * width), BF)], hidden, deltas, *w_in, *w_out, fetch=10
    )
    back, deltas_got = lax.optimization_barrier((back, deltas_got))
    back = swap(back.reshape(EXPERTS, CAP, 2 * width), OWN).reshape(slots, 2 * width)

    shape = (width, 2 * hs)
    in_keep, in_away = local(
        in_kernel, [(shape, F32), (shape, BF)], rows, rows_next, deltas, deltas_got
    )
    factor = 1.0 / math.sqrt(8 * tok_rows)
    in_grad = (in_keep + swap_pair(in_away, "zb").astype(F32)) * factor
    gate_grad, up_grad = in_grad[:, :hs], in_grad[:, hs:]
    down_grad = (down_keep + down_got.astype(F32)) * factor
    mixed, tokens_grad = local(home_kernel, [((tok_rows, width), F32)] * 2, ids, weight, back)
    return (mixed, tokens_grad, gate_grad[None], up_grad[None], down_grad.T[None])


def solution(mesh):
    fine = Mesh(mesh.devices.reshape(8, 2, 4, 4, 2, 2), GRP + EP)
    return jax.shard_map(
        body,
        mesh=fine,
        in_specs=(
            P(EP, GRP),
            P(EP, None),
            P(EP, None),
            P(EP, GRP),
            P(EP, GRP, None),
            P(EP, GRP, None),
            P(EP, None, GRP),
        ),
        out_specs=(
            P(EP, GRP),
            P(EP, GRP),
            P(EP, GRP, None),
            P(EP, GRP, None),
            P(EP, None, GRP),
        ),
        check_vma=False,
    )
```

```python
import math

import jax
import jax.numpy as jnp
from jax import lax
from jax.experimental import pallas as pl
from jax.experimental.pallas import tpu as pltpu
from jax.sharding import Mesh, PartitionSpec as P

TOP = 2
CAP = 16
EXPERTS = 16
SLICES = 4
OWN = ("x", "zp")
SLICE = ("zb", "c")
EP = OWN + SLICE
GRP = ("y", "zh")

PLAIN = (((1,), (0,)), ((), ()))
LAST = (((1,), (1,)), ((), ()))
FIRST = (((0,), (0,)), ((), ()))
F32 = jnp.float32
BF = jnp.bfloat16


def dot(a, b, dims=PLAIN):
    return lax.dot_general(a, b, dims, preferred_element_type=F32)


def local(kernel, outs, *args, fetch=0):
    size = sum(a.size * a.dtype.itemsize for a in args)
    size += sum(math.prod(shape) * jnp.dtype(kind).itemsize for shape, kind in outs)
    stay, total = len(args) - fetch, len(args)

    def fetching(*refs):
        results = refs[total : total + len(outs)]
        held, sems = refs[total + len(outs) : -1], refs[-1]
        moves = [
            pltpu.make_async_copy(refs[stay + i], held[i], sems.at[i]) for i in range(fetch)
        ]
        for move in moves:
            move.start()
        for move in moves:
            move.wait()
        kernel(*refs[:stay], *held, *results)

    scratch = [pltpu.VMEM(a.shape, a.dtype) for a in args[stay:]]
    return pl.pallas_call(
        fetching if fetch else kernel,
        out_shape=[jax.ShapeDtypeStruct(shape, kind) for shape, kind in outs],
        in_specs=[pl.BlockSpec(memory_space=pltpu.VMEM)] * stay
        + [pl.BlockSpec(memory_space=pltpu.HBM)] * fetch,
        out_specs=[pl.BlockSpec(memory_space=pltpu.VMEM)] * len(outs),
        scratch_shapes=scratch + [pltpu.SemaphoreType.DMA((fetch,))] if fetch else (),
        compiler_params=pltpu.CompilerParams(vmem_limit_bytes=(56 if fetch else 16) * 2**20),
        cost_estimate=pl.CostEstimate(
            flops=2 * 10**9, bytes_accessed=2 * size, transcendentals=0
        ),
    )(*args)


def pair(ref):
    return jnp.concatenate([ref[0:1], ref[1:2]], axis=1)


def hits(ids_ref):
    ids = pair(ids_ref)
    count = ids.shape[1]
    across = jnp.broadcast_to(ids, (count, count))
    first = lax.broadcasted_iota(jnp.int32, (count, count), 0)
    second = lax.broadcasted_iota(jnp.int32, (count, count), 1)
    earlier = (across.T == across) & (first < second)
    rank = jnp.sum(jnp.where(earlier, 1.0, 0.0), axis=0, keepdims=True)
    target = ids * CAP + rank.astype(jnp.int32)
    return lax.broadcasted_iota(jnp.int32, (EXPERTS * CAP, count), 0) == target


def pack_kernel(ids_ref, weight_ref, tokens_ref, grad_ref, send_ref):
    hit = hits(ids_ref)
    slot_weight = jnp.sum(jnp.where(hit, pair(weight_ref), 0.0), axis=1, keepdims=True)
    place = jnp.where(hit, 1.0, 0.0).astype(BF)
    tokens = tokens_ref[...]
    grads = grad_ref[...]
    rows = dot(place, jnp.concatenate([tokens, tokens], axis=0))
    grad_rows = slot_weight * dot(place, jnp.concatenate([grads, grads], axis=0))
    send_ref[...] = jnp.concatenate([rows, grad_rows], axis=1).astype(BF)


def pre_kernel(rows_ref, *refs):
    out_ref = refs[-1]
    width, hs = refs[0].shape[0], refs[0].shape[1] // 2
    half = out_ref.shape[1] // 2
    rows = rows_ref[:, :width]
    for s in range(SLICES):
        both = dot(rows, refs[s][...]).astype(BF)
        out_ref[:, s * hs : (s + 1) * hs] = both[:, :hs]
        out_ref[:, half + s * hs : half + (s + 1) * hs] = both[:, hs:]


def act_kernel(rows_ref, *refs):
    out_ref = refs[-1]
    width, hs = refs[0].shape
    rows = rows_ref[:, width:]
    for s in range(SLICES):
        out_ref[:, s * hs : (s + 1) * hs] = dot(rows, refs[s][...]).astype(BF)


def sum_kernel(got_ref, sum_ref, round_ref):
    total = jnp.sum(got_ref[...].astype(F32), axis=0)
    sum_ref[...] = total
    round_ref[...] = total.astype(BF)


def hidden_kernel(part_ref, other_ref, hidden_ref):
    units = part_ref.shape[1] // 2
    pre = part_ref[...] + other_ref[...].astype(F32)
    gate_pre, up_pre = pre[:, :units], pre[:, units:]
    hidden = (gate_pre * jax.nn.sigmoid(gate_pre) * up_pre).astype(BF)
    hidden_ref[...] = jnp.broadcast_to(hidden[None], hidden_ref.shape)


def delta_kernel(part_ref, other_ref, act_ref, act_other_ref, delta_ref):
    units = act_ref.shape[1]
    pre = part_ref[...] + other_ref[...].astype(F32)
    act_grad = act_ref[...] + act_other_ref[...].astype(F32)
    gate_pre, up_pre = pre[:, :units], pre[:, units:]
    sig = jax.nn.sigmoid(gate_pre)
    gate_delta = act_grad * up_pre * sig * (1.0 + gate_pre * (1.0 - sig))
    up_delta = act_grad * gate_pre * sig
    shape = (delta_ref.shape[0],) + act_ref.shape
    delta_ref[:, :, :units] = jnp.broadcast_to(gate_delta.astype(BF)[None], shape)
    delta_ref[:, :, units:] = jnp.broadcast_to(up_delta.astype(BF)[None], shape)


def back_kernel(hidden_ref, deltas_ref, *refs):
    out_ref = refs[-1]
    in_refs, down_refs = refs[:SLICES], refs[SLICES:-1]
    hs = down_refs[0].shape[1]
    half = deltas_ref.shape[1] // 2
    out_rows = in_rows = 0.0
    for s in range(SLICES):
        here = slice(s * hs, (s + 1) * hs)
        there = slice(half + s * hs, half + (s + 1) * hs)
        out_rows += dot(hidden_ref[:, here], down_refs[s][...], LAST)
        both = jnp.concatenate([deltas_ref[:, here], deltas_ref[:, there]], axis=1)
        in_rows += dot(both, in_refs[s][...], LAST)
    out_ref[...] = jnp.concatenate([out_rows, in_rows], axis=1).astype(BF)


def down_kernel(rows_ref, next_ref, own_ref, got_ref, keep_ref, away_ref):
    width, hs = keep_ref.shape
    rows, following = rows_ref[:, width:], next_ref[:, width:]
    for step, out_ref in ((0, keep_ref), (2, away_ref)):
        there = slice(step // 2 * hs, (step // 2 + 1) * hs)
        total = dot(rows, own_ref[:, step * hs : (step + 1) * hs], FIRST)
        total += dot(following, got_ref[:, there], FIRST)
        out_ref[...] = total.astype(out_ref.dtype)


def in_kernel(factor, rows_ref, next_ref, own_ref, got_ref, keep_ref, away_ref):
    width, hs = keep_ref.shape[0], keep_ref.shape[1] // 2
    half = own_ref.shape[1] // 2
    rows, following = rows_ref[:, :width], next_ref[:, :width]
    for step, out_ref in ((0, keep_ref), (2, away_ref)):
        for side in (0, 1):
            here = slice(side * half + step * hs, side * half + (step + 1) * hs)
            there = slice((step + side) * hs, (step + side + 1) * hs)
            total = dot(rows, own_ref[:, here], FIRST)
            total += dot(following, got_ref[:, there], FIRST)
            out_ref[:, side * hs : (side + 1) * hs] = (total * factor).astype(out_ref.dtype)


def join_kernel(keep_ref, got_ref, *grad_refs):
    total = keep_ref[...] + got_ref[...].astype(F32)
    hs = grad_refs[0].shape[1]
    for side, grad_ref in enumerate(grad_refs):
        grad_ref[...] = total[:, side * hs : (side + 1) * hs]


def place_kernel(ids_ref, weight_ref, place_ref, column_ref):
    place_ref[...] = jnp.where(hits(ids_ref), 1.0, 0.0).astype(BF)
    row = pair(weight_ref)
    count = row.shape[1]
    column_ref[...] = jnp.broadcast_to(row, (count, count)).T


def home_kernel(place_ref, weight_ref, back_ref, mixed_ref, grad_ref):
    tok_rows, width = mixed_ref.shape
    per = dot(place_ref[...], back_ref[...], FIRST)
    per_out = per[:, :width] * weight_ref[:, :1]
    per_in = per[:, width:]
    mixed_ref[...] = per_out[:tok_rows] + per_out[tok_rows:]
    grad_ref[...] = per_in[:tok_rows] + per_in[tok_rows:]


def swap(value, axis):
    return lax.all_to_all(value, axis, split_axis=0, concat_axis=0, tiled=True)


def sum_y(part):
    rows, cols = part.shape
    got = swap(part.reshape(8, rows // 8, cols), "y")
    shape = (rows // 8, cols)
    return local(sum_kernel, [(shape, F32), (shape, BF)], got)


def swap_pair(value, axis):
    return lax.ppermute(value, axis, [(0, 1), (1, 0)])


def gather_y(copies):
    count, rows, cols = copies.shape
    return swap(copies, "y").reshape(count * rows, cols)


def share(value):
    across = swap_pair(value, "zb")
    return [value, swap_pair(value, "c"), across, swap_pair(across, "c")]


def body(tokens, expert_ids, route_weight, out_grad, w_gate, w_up, w_down):
    tok_rows, width = tokens.shape
    hs = w_gate.shape[2]
    units = SLICES * hs
    slots = EXPERTS * CAP
    ids, weight = expert_ids.T, route_weight.T
    (send,) = local(
        pack_kernel, [((slots, 2 * width), BF)], ids, weight, tokens, out_grad, fetch=4
    )
    send, w_gate, w_up = lax.optimization_barrier((send, w_gate, w_up))
    rows = swap(send.reshape(EXPERTS, CAP, 2 * width), OWN).reshape(slots, 2 * width)
    w_in = share(jnp.concatenate([w_gate[0], w_up[0]], axis=1))
    (pre_local,) = local(pre_kernel, [((slots, 2 * units), BF)], rows, *w_in)
    pre_local, rows, w_down = lax.optimization_barrier((pre_local, rows, w_down))
    pre_part, pre_round = sum_y(pre_local)
    w_out = share(w_down[0].T)
    rows_next = swap_pair(rows, "c")
    (act_local,) = local(act_kernel, [((slots, units), BF)], rows, *w_out)
    act_local, rows_next = lax.optimization_barrier((act_local, rows_next))
    act_part, act_round = sum_y(act_local)

    pre_other = swap_pair(pre_round, "zh")
    copies = (8, slots // 8)
    (hidden,) = local(hidden_kernel, [(copies + (units,), BF)], pre_part, pre_other)
    hidden, act_round = lax.optimization_barrier((hidden, act_round))
    hidden = gather_y(hidden)
    act_other = swap_pair(act_round, "zh")
    (deltas,) = local(
        delta_kernel, [(copies + (2 * units,), BF)], pre_part, pre_other, act_part, act_other
    )
    deltas = gather_y(deltas)

    def to_next(value):
        sides = value.shape[1] // units
        cut = [
            value[:, side * units + step * hs :][:, :hs] for step in (1, 3) for side in range(sides)
        ]
        return swap_pair(jnp.concatenate(cut, axis=1), "c")

    shape = (width, hs)
    down_keep, down_away = local(
        down_kernel, [(shape, F32), (shape, BF)], rows, rows_next, hidden, to_next(hidden)
    )
    down_got = swap_pair(down_away, "zb")
    deltas, hidden, down_got = lax.optimization_barrier((deltas, hidden, down_got))
    deltas_got = to_next(deltas)
    (back,) = local(
        back_kernel, [((slots, 2 * width), BF)], hidden, deltas, *w_in, *w_out
    )
    back, deltas_got, ids, weight = lax.optimization_barrier((back, deltas_got, ids, weight))
    count = TOP * tok_rows
    place, column = local(
        place_kernel, [((slots, count), BF), ((count, count), F32)], ids, weight
    )
    back = swap(back.reshape(EXPERTS, CAP, 2 * width), OWN).reshape(slots, 2 * width)

    factor = 1.0 / math.sqrt(8 * tok_rows)

    def into(*refs):
        in_kernel(factor, *refs)

    shape = (width, 2 * hs)
    in_keep, in_away = local(
        into, [(shape, F32), (shape, BF)], rows, rows_next, deltas, deltas_got
    )
    gate_grad, up_grad = local(
        join_kernel, [((width, hs), F32)] * 2, in_keep, swap_pair(in_away, "zb")
    )
    down_grad = (down_keep + down_got.astype(F32)) * factor
    mixed, tokens_grad = local(home_kernel, [((tok_rows, width), F32)] * 2, place, column, back)
    return (mixed, tokens_grad, gate_grad[None], up_grad[None], down_grad.T[None])


def solution(mesh):
    fine = Mesh(mesh.devices.reshape(8, 2, 4, 4, 2, 2), GRP + EP)
    return jax.shard_map(
        body,
        mesh=fine,
        in_specs=(
            P(EP, GRP),
            P(EP, None),
            P(EP, None),
            P(EP, GRP),
            P(EP, GRP, None),
            P(EP, GRP, None),
            P(EP, None, GRP),
        ),
        out_specs=(
            P(EP, GRP),
            P(EP, GRP),
            P(EP, GRP, None),
            P(EP, GRP, None),
            P(EP, None, GRP),
        ),
        check_vma=False,
    )
```

```python
import math

import jax
import jax.numpy as jnp
from jax import lax
from jax.experimental import pallas as pl
from jax.experimental.pallas import tpu as pltpu
from jax.sharding import Mesh, PartitionSpec as P

TOP = 2
CAP = 16
EXPERTS = 16
SLICES = 4
OWN = ("x", "zp")
SLICE = ("zb", "c")
EP = OWN + SLICE
GRP = ("y", "zh")

PLAIN = (((1,), (0,)), ((), ()))
LAST = (((1,), (1,)), ((), ()))
FIRST = (((0,), (0,)), ((), ()))
F32 = jnp.float32
BF = jnp.bfloat16


def dot(a, b, dims=PLAIN):
    return lax.dot_general(a, b, dims, preferred_element_type=F32)


def local(kernel, outs, *args, fetch=0):
    size = sum(a.size * a.dtype.itemsize for a in args)
    size += sum(math.prod(shape) * jnp.dtype(kind).itemsize for shape, kind in outs)
    stay, total = len(args) - fetch, len(args)

    def fetching(*refs):
        results = refs[total : total + len(outs)]
        held, sems = refs[total + len(outs) : -1], refs[-1]
        moves = [
            pltpu.make_async_copy(refs[stay + i], held[i], sems.at[i]) for i in range(fetch)
        ]
        for move in moves:
            move.start()
        for move in moves:
            move.wait()
        kernel(*refs[:stay], *held, *results)

    scratch = [pltpu.VMEM(a.shape, a.dtype) for a in args[stay:]]
    return pl.pallas_call(
        fetching if fetch else kernel,
        out_shape=[jax.ShapeDtypeStruct(shape, kind) for shape, kind in outs],
        in_specs=[pl.BlockSpec(memory_space=pltpu.VMEM)] * stay
        + [pl.BlockSpec(memory_space=pltpu.HBM)] * fetch,
        out_specs=[pl.BlockSpec(memory_space=pltpu.VMEM)] * len(outs),
        scratch_shapes=scratch + [pltpu.SemaphoreType.DMA((fetch,))] if fetch else (),
        compiler_params=pltpu.CompilerParams(vmem_limit_bytes=(56 if fetch else 16) * 2**20),
        cost_estimate=pl.CostEstimate(
            flops=2 * 10**9, bytes_accessed=2 * size, transcendentals=0
        ),
    )(*args)


def pair(ref):
    return jnp.concatenate([ref[0:1], ref[1:2]], axis=1)


def hits(ids_ref):
    ids = pair(ids_ref)
    count = ids.shape[1]
    across = jnp.broadcast_to(ids, (count, count))
    first = lax.broadcasted_iota(jnp.int32, (count, count), 0)
    second = lax.broadcasted_iota(jnp.int32, (count, count), 1)
    earlier = (across.T == across) & (first < second)
    rank = jnp.sum(jnp.where(earlier, 1.0, 0.0), axis=0, keepdims=True)
    target = ids * CAP + rank.astype(jnp.int32)
    return lax.broadcasted_iota(jnp.int32, (EXPERTS * CAP, count), 0) == target


def pack_kernel(ids_ref, weight_ref, tokens_ref, grad_ref, send_ref):
    hit = hits(ids_ref)
    slot_weight = jnp.sum(jnp.where(hit, pair(weight_ref), 0.0), axis=1, keepdims=True)
    place = jnp.where(hit, 1.0, 0.0).astype(BF)
    tokens = tokens_ref[...]
    grads = grad_ref[...]
    rows = dot(place, jnp.concatenate([tokens, tokens], axis=0))
    grad_rows = slot_weight * dot(place, jnp.concatenate([grads, grads], axis=0))
    send_ref[...] = jnp.concatenate([rows, grad_rows], axis=1).astype(BF)


def pre_kernel(rows_ref, *refs):
    out_ref = refs[-1]
    width, hs = refs[0].shape[0], refs[0].shape[1] // 2
    half = out_ref.shape[1] // 2
    rows = rows_ref[:, :width]
    for s in range(SLICES):
        both = dot(rows, refs[s][...]).astype(BF)
        out_ref[:, s * hs : (s + 1) * hs] = both[:, :hs]
        out_ref[:, half + s * hs : half + (s + 1) * hs] = both[:, hs:]


def act_kernel(rows_ref, *refs):
    out_ref = refs[-1]
    width, hs = refs[0].shape
    rows = rows_ref[:, width:]
    for s in range(SLICES):
        out_ref[:, s * hs : (s + 1) * hs] = dot(rows, refs[s][...]).astype(BF)


def sum_kernel(got_ref, sum_ref):
    sum_ref[...] = jnp.sum(got_ref[...].astype(F32), axis=0).astype(BF)


def hidden_kernel(part_ref, other_ref, hidden_ref):
    units = part_ref.shape[1] // 2
    pre = part_ref[...].astype(F32) + other_ref[...].astype(F32)
    gate_pre, up_pre = pre[:, :units], pre[:, units:]
    hidden = (gate_pre * jax.nn.sigmoid(gate_pre) * up_pre).astype(BF)
    hidden_ref[...] = jnp.broadcast_to(hidden[None], hidden_ref.shape)


def delta_kernel(part_ref, other_ref, act_ref, act_other_ref, delta_ref):
    units = act_ref.shape[1]
    pre = part_ref[...].astype(F32) + other_ref[...].astype(F32)
    act_grad = act_ref[...].astype(F32) + act_other_ref[...].astype(F32)
    gate_pre, up_pre = pre[:, :units], pre[:, units:]
    sig = jax.nn.sigmoid(gate_pre)
    gate_delta = act_grad * up_pre * sig * (1.0 + gate_pre * (1.0 - sig))
    up_delta = act_grad * gate_pre * sig
    shape = (delta_ref.shape[0],) + act_ref.shape
    delta_ref[:, :, :units] = jnp.broadcast_to(gate_delta.astype(BF)[None], shape)
    delta_ref[:, :, units:] = jnp.broadcast_to(up_delta.astype(BF)[None], shape)


def back_kernel(hidden_ref, deltas_ref, *refs):
    out_ref = refs[-1]
    in_refs, down_refs = refs[:SLICES], refs[SLICES:-1]
    hs = down_refs[0].shape[1]
    half = deltas_ref.shape[1] // 2
    out_rows = in_rows = 0.0
    for s in range(SLICES):
        here = slice(s * hs, (s + 1) * hs)
        there = slice(half + s * hs, half + (s + 1) * hs)
        out_rows += dot(hidden_ref[:, here], down_refs[s][...], LAST)
        both = jnp.concatenate([deltas_ref[:, here], deltas_ref[:, there]], axis=1)
        in_rows += dot(both, in_refs[s][...], LAST)
    out_ref[...] = jnp.concatenate([out_rows, in_rows], axis=1).astype(BF)


def down_kernel(rows_ref, next_ref, own_ref, got_ref, keep_ref, away_ref):
    width, hs = keep_ref.shape
    rows, following = rows_ref[:, width:], next_ref[:, width:]
    for step, out_ref in ((0, keep_ref), (2, away_ref)):
        there = slice(step // 2 * hs, (step // 2 + 1) * hs)
        total = dot(rows, own_ref[:, step * hs : (step + 1) * hs], FIRST)
        total += dot(following, got_ref[:, there], FIRST)
        out_ref[...] = total.astype(out_ref.dtype)


def in_kernel(factor, rows_ref, next_ref, own_ref, got_ref, keep_ref, away_ref):
    width, hs = keep_ref.shape[0], keep_ref.shape[1] // 2
    half = own_ref.shape[1] // 2
    rows, following = rows_ref[:, :width], next_ref[:, :width]
    for step, out_ref in ((0, keep_ref), (2, away_ref)):
        for side in (0, 1):
            here = slice(side * half + step * hs, side * half + (step + 1) * hs)
            there = slice((step + side) * hs, (step + side + 1) * hs)
            total = dot(rows, own_ref[:, here], FIRST)
            total += dot(following, got_ref[:, there], FIRST)
            out_ref[:, side * hs : (side + 1) * hs] = (total * factor).astype(out_ref.dtype)


def join_kernel(keep_ref, got_ref, *grad_refs):
    total = keep_ref[...] + got_ref[...].astype(F32)
    hs = grad_refs[0].shape[1]
    for side, grad_ref in enumerate(grad_refs):
        grad_ref[...] = total[:, side * hs : (side + 1) * hs]


def place_kernel(ids_ref, weight_ref, place_ref, column_ref):
    place_ref[...] = jnp.where(hits(ids_ref), 1.0, 0.0).astype(BF)
    row = pair(weight_ref)
    count = row.shape[1]
    column_ref[...] = jnp.broadcast_to(row, (count, count)).T


def home_kernel(place_ref, weight_ref, back_ref, mixed_ref, grad_ref):
    tok_rows, width = mixed_ref.shape
    per = dot(place_ref[...], back_ref[...], FIRST)
    per_out = per[:, :width] * weight_ref[:, :1]
    per_in = per[:, width:]
    mixed_ref[...] = per_out[:tok_rows] + per_out[tok_rows:]
    grad_ref[...] = per_in[:tok_rows] + per_in[tok_rows:]


def swap(value, axis):
    return lax.all_to_all(value, axis, split_axis=0, concat_axis=0, tiled=True)


def sum_y(part):
    rows, cols = part.shape
    got = swap(part.reshape(8, rows // 8, cols), "y")
    (total,) = local(sum_kernel, [((rows // 8, cols), BF)], got)
    return total


def swap_pair(value, axis):
    return lax.ppermute(value, axis, [(0, 1), (1, 0)])


def gather_y(copies):
    count, rows, cols = copies.shape
    return swap(copies, "y").reshape(count * rows, cols)


def share(value):
    across = swap_pair(value, "zb")
    return [value, swap_pair(value, "c"), across, swap_pair(across, "c")]


def body(tokens, expert_ids, route_weight, out_grad, w_gate, w_up, w_down):
    tok_rows, width = tokens.shape
    hs = w_gate.shape[2]
    units = SLICES * hs
    slots = EXPERTS * CAP
    ids, weight = expert_ids.T, route_weight.T
    (send,) = local(
        pack_kernel, [((slots, 2 * width), BF)], ids, weight, tokens, out_grad, fetch=4
    )
    send, w_gate, w_up = lax.optimization_barrier((send, w_gate, w_up))
    rows = swap(send.reshape(EXPERTS, CAP, 2 * width), OWN).reshape(slots, 2 * width)
    w_in = share(jnp.concatenate([w_gate[0], w_up[0]], axis=1))
    (pre_local,) = local(pre_kernel, [((slots, 2 * units), BF)], rows, *w_in)
    pre_local, rows, w_down = lax.optimization_barrier((pre_local, rows, w_down))
    pre_part = sum_y(pre_local)
    w_out = share(w_down[0].T)
    rows_next = swap_pair(rows, "c")
    (act_local,) = local(act_kernel, [((slots, units), BF)], rows, *w_out)
    act_local, rows_next = lax.optimization_barrier((act_local, rows_next))
    act_part = sum_y(act_local)

    pre_other = swap_pair(pre_part, "zh")
    copies = (8, slots // 8)
    (hidden,) = local(hidden_kernel, [(copies + (units,), BF)], pre_part, pre_other)
    hidden, act_part = lax.optimization_barrier((hidden, act_part))
    hidden = gather_y(hidden)
    act_other = swap_pair(act_part, "zh")
    (deltas,) = local(
        delta_kernel, [(copies + (2 * units,), BF)], pre_part, pre_other, act_part, act_other
    )
    deltas = gather_y(deltas)

    def to_next(value):
        sides = value.shape[1] // units
        cut = [
            value[:, side * units + step * hs :][:, :hs] for step in (1, 3) for side in range(sides)
        ]
        return swap_pair(jnp.concatenate(cut, axis=1), "c")

    shape = (width, hs)
    down_keep, down_away = local(
        down_kernel, [(shape, F32), (shape, BF)], rows, rows_next, hidden, to_next(hidden)
    )
    down_got = swap_pair(down_away, "zb")
    deltas, hidden, down_got = lax.optimization_barrier((deltas, hidden, down_got))
    deltas_got = to_next(deltas)
    (back,) = local(
        back_kernel, [((slots, 2 * width), BF)], hidden, deltas, *w_in, *w_out
    )
    back, deltas_got, ids, weight = lax.optimization_barrier((back, deltas_got, ids, weight))
    count = TOP * tok_rows
    place, column = local(
        place_kernel, [((slots, count), BF), ((count, count), F32)], ids, weight
    )
    back = swap(back.reshape(EXPERTS, CAP, 2 * width), OWN).reshape(slots, 2 * width)

    factor = 1.0 / math.sqrt(8 * tok_rows)

    def into(*refs):
        in_kernel(factor, *refs)

    shape = (width, 2 * hs)
    in_keep, in_away = local(
        into, [(shape, F32), (shape, BF)], rows, rows_next, deltas, deltas_got
    )
    gate_grad, up_grad = local(
        join_kernel, [((width, hs), F32)] * 2, in_keep, swap_pair(in_away, "zb")
    )
    down_grad = (down_keep + down_got.astype(F32)) * factor
    mixed, tokens_grad = local(home_kernel, [((tok_rows, width), F32)] * 2, place, column, back)
    return (mixed, tokens_grad, gate_grad[None], up_grad[None], down_grad.T[None])


def solution(mesh):
    fine = Mesh(mesh.devices.reshape(8, 2, 4, 4, 2, 2), GRP + EP)
    return jax.shard_map(
        body,
        mesh=fine,
        in_specs=(
            P(EP, GRP),
            P(EP, None),
            P(EP, None),
            P(EP, GRP),
            P(EP, GRP, None),
            P(EP, GRP, None),
            P(EP, None, GRP),
        ),
        out_specs=(
            P(EP, GRP),
            P(EP, GRP),
            P(EP, GRP, None),
            P(EP, GRP, None),
            P(EP, None, GRP),
        ),
        check_vma=False,
    )
```

```python
import math

import jax
import jax.numpy as jnp
from jax import lax
from jax.experimental import pallas as pl
from jax.experimental.pallas import tpu as pltpu
from jax.sharding import Mesh, PartitionSpec as P

TOP = 2
CAP = 16
EXPERTS = 16
SLICES = 4
OWN = ("x", "zp")
SLICE = ("zb", "c")
EP = OWN + SLICE
GRP = ("y", "zh")

PLAIN = (((1,), (0,)), ((), ()))
LAST = (((1,), (1,)), ((), ()))
FIRST = (((0,), (0,)), ((), ()))
F32 = jnp.float32
BF = jnp.bfloat16


def dot(a, b, dims=PLAIN):
    return lax.dot_general(a, b, dims, preferred_element_type=F32)


def local(kernel, outs, *args, fetch=0):
    size = sum(a.size * a.dtype.itemsize for a in args)
    size += sum(math.prod(shape) * jnp.dtype(kind).itemsize for shape, kind in outs)
    stay, total = len(args) - fetch, len(args)

    def fetching(*refs):
        results = refs[total : total + len(outs)]
        held, sems = refs[total + len(outs) : -1], refs[-1]
        moves = [
            pltpu.make_async_copy(refs[stay + i], held[i], sems.at[i]) for i in range(fetch)
        ]
        for move in moves:
            move.start()
        for move in moves:
            move.wait()
        kernel(*refs[:stay], *held, *results)

    scratch = [pltpu.VMEM(a.shape, a.dtype) for a in args[stay:]]
    return pl.pallas_call(
        fetching if fetch else kernel,
        out_shape=[jax.ShapeDtypeStruct(shape, kind) for shape, kind in outs],
        in_specs=[pl.BlockSpec(memory_space=pltpu.VMEM)] * stay
        + [pl.BlockSpec(memory_space=pltpu.HBM)] * fetch,
        out_specs=[pl.BlockSpec(memory_space=pltpu.VMEM)] * len(outs),
        scratch_shapes=scratch + [pltpu.SemaphoreType.DMA((fetch,))] if fetch else (),
        compiler_params=pltpu.CompilerParams(vmem_limit_bytes=(56 if fetch else 16) * 2**20),
        cost_estimate=pl.CostEstimate(
            flops=2 * 10**9, bytes_accessed=2 * size, transcendentals=0
        ),
    )(*args)


def pair(ref):
    return jnp.concatenate([ref[0:1], ref[1:2]], axis=1)


def hits(ids_ref):
    ids = pair(ids_ref)
    count = ids.shape[1]
    across = jnp.broadcast_to(ids, (count, count))
    first = lax.broadcasted_iota(jnp.int32, (count, count), 0)
    second = lax.broadcasted_iota(jnp.int32, (count, count), 1)
    earlier = (across.T == across) & (first < second)
    rank = jnp.sum(jnp.where(earlier, 1.0, 0.0), axis=0, keepdims=True)
    target = ids * CAP + rank.astype(jnp.int32)
    return lax.broadcasted_iota(jnp.int32, (EXPERTS * CAP, count), 0) == target


def pack_kernel(ids_ref, weight_ref, tokens_ref, grad_ref, send_ref):
    hit = hits(ids_ref)
    slot_weight = jnp.sum(jnp.where(hit, pair(weight_ref), 0.0), axis=1, keepdims=True)
    place = jnp.where(hit, 1.0, 0.0).astype(BF)
    tokens = tokens_ref[...]
    grads = grad_ref[...]
    rows = dot(place, jnp.concatenate([tokens, tokens], axis=0))
    grad_rows = slot_weight * dot(place, jnp.concatenate([grads, grads], axis=0))
    send_ref[...] = jnp.concatenate([rows, grad_rows], axis=1).astype(BF)


def pre_kernel(rows_ref, *refs):
    out_ref = refs[-1]
    width, hs = refs[0].shape[0], refs[0].shape[1] // 2
    half = out_ref.shape[1] // 2
    rows = rows_ref[:, :width]
    for s in range(SLICES):
        both = dot(rows, refs[s][...]).astype(BF)
        out_ref[:, s * hs : (s + 1) * hs] = both[:, :hs]
        out_ref[:, half + s * hs : half + (s + 1) * hs] = both[:, hs:]


def act_kernel(rows_ref, *refs):
    out_ref = refs[-1]
    width, hs = refs[0].shape
    rows = rows_ref[:, width:]
    for s in range(SLICES):
        out_ref[:, s * hs : (s + 1) * hs] = dot(rows, refs[s][...]).astype(BF)


def sum_kernel(got_ref, sum_ref):
    sum_ref[...] = jnp.sum(got_ref[...].astype(F32), axis=0).astype(BF)


def hidden_kernel(part_ref, other_ref, hidden_ref):
    units = part_ref.shape[1] // 2
    pre = part_ref[...].astype(F32) + other_ref[...].astype(F32)
    gate_pre, up_pre = pre[:, :units], pre[:, units:]
    hidden = (gate_pre * jax.nn.sigmoid(gate_pre) * up_pre).astype(BF)
    hidden_ref[...] = jnp.broadcast_to(hidden[None], hidden_ref.shape)


def delta_kernel(part_ref, other_ref, act_ref, act_other_ref, delta_ref):
    units = act_ref.shape[1]
    pre = part_ref[...].astype(F32) + other_ref[...].astype(F32)
    act_grad = act_ref[...].astype(F32) + act_other_ref[...].astype(F32)
    gate_pre, up_pre = pre[:, :units], pre[:, units:]
    sig = jax.nn.sigmoid(gate_pre)
    gate_delta = act_grad * up_pre * sig * (1.0 + gate_pre * (1.0 - sig))
    up_delta = act_grad * gate_pre * sig
    shape = (delta_ref.shape[0],) + act_ref.shape
    delta_ref[:, :, :units] = jnp.broadcast_to(gate_delta.astype(BF)[None], shape)
    delta_ref[:, :, units:] = jnp.broadcast_to(up_delta.astype(BF)[None], shape)


def back_kernel(hidden_ref, deltas_ref, *refs):
    out_ref = refs[-1]
    in_refs, down_refs = refs[:SLICES], refs[SLICES:-1]
    hs = down_refs[0].shape[1]
    half = deltas_ref.shape[1] // 2
    out_rows = in_rows = 0.0
    for s in range(SLICES):
        here = slice(s * hs, (s + 1) * hs)
        there = slice(half + s * hs, half + (s + 1) * hs)
        out_rows += dot(hidden_ref[:, here], down_refs[s][...], LAST)
        both = jnp.concatenate([deltas_ref[:, here], deltas_ref[:, there]], axis=1)
        in_rows += dot(both, in_refs[s][...], LAST)
    out_ref[...] = jnp.concatenate([out_rows, in_rows], axis=1).astype(BF)


def down_kernel(rows_ref, next_ref, own_ref, got_ref, keep_ref, away_ref):
    width, hs = keep_ref.shape
    rows, following = rows_ref[:, width:], next_ref[:, width:]
    for step, out_ref in ((0, keep_ref), (2, away_ref)):
        there = slice(step // 2 * hs, (step // 2 + 1) * hs)
        total = dot(rows, own_ref[:, step * hs : (step + 1) * hs], FIRST)
        total += dot(following, got_ref[:, there], FIRST)
        out_ref[...] = total.astype(out_ref.dtype)


def in_kernel(factor, rows_ref, next_ref, own_ref, got_ref, keep_ref, away_ref):
    width, hs = keep_ref.shape[0], keep_ref.shape[1] // 2
    half = own_ref.shape[1] // 2
    rows, following = rows_ref[:, :width], next_ref[:, :width]
    for step, out_ref in ((0, keep_ref), (2, away_ref)):
        for side in (0, 1):
            here = slice(side * half + step * hs, side * half + (step + 1) * hs)
            there = slice((step + side) * hs, (step + side + 1) * hs)
            total = dot(rows, own_ref[:, here], FIRST)
            total += dot(following, got_ref[:, there], FIRST)
            out_ref[:, side * hs : (side + 1) * hs] = (total * factor).astype(out_ref.dtype)


def join_kernel(keep_ref, got_ref, *grad_refs):
    total = keep_ref[...] + got_ref[...].astype(F32)
    hs = grad_refs[0].shape[1]
    for side, grad_ref in enumerate(grad_refs):
        grad_ref[...] = total[:, side * hs : (side + 1) * hs]


def place_kernel(ids_ref, weight_ref, place_ref, column_ref):
    place_ref[...] = jnp.where(hits(ids_ref), 1.0, 0.0).astype(BF)
    row = pair(weight_ref)
    count = row.shape[1]
    column_ref[...] = jnp.broadcast_to(row, (count, count)).T


def home_kernel(place_ref, weight_ref, back_ref, mixed_ref, grad_ref):
    tok_rows, width = mixed_ref.shape
    per = dot(place_ref[...], back_ref[...], FIRST)
    per_out = per[:, :width] * weight_ref[:, :1]
    per_in = per[:, width:]
    mixed_ref[...] = per_out[:tok_rows] + per_out[tok_rows:]
    grad_ref[...] = per_in[:tok_rows] + per_in[tok_rows:]


def swap(value, axis):
    return lax.all_to_all(value, axis, split_axis=0, concat_axis=0, tiled=True)


def sum_y(part):
    rows, cols = part.shape
    got = swap(part.reshape(8, rows // 8, cols), "y")
    (total,) = local(sum_kernel, [((rows // 8, cols), BF)], got)
    return total


def swap_pair(value, axis):
    return lax.ppermute(value, axis, [(0, 1), (1, 0)])


def gather_y(copies):
    count, rows, cols = copies.shape
    return swap(copies, "y").reshape(count * rows, cols)


def share(value):
    across = swap_pair(value, "zb")
    return [value, swap_pair(value, "c"), across, swap_pair(across, "c")]


def body(tokens, expert_ids, route_weight, out_grad, w_gate, w_up, w_down):
    tok_rows, width = tokens.shape
    hs = w_gate.shape[2]
    units = SLICES * hs
    slots = EXPERTS * CAP
    ids, weight = expert_ids.T, route_weight.T
    (send,) = local(
        pack_kernel, [((slots, 2 * width), BF)], ids, weight, tokens, out_grad, fetch=4
    )
    send, w_gate, w_up = lax.optimization_barrier((send, w_gate, w_up))
    rows = swap(send.reshape(EXPERTS, CAP, 2 * width), OWN).reshape(slots, 2 * width)
    w_in = share(jnp.concatenate([w_gate[0], w_up[0]], axis=1))
    (pre_local,) = local(pre_kernel, [((slots, 2 * units), BF)], rows, *w_in)
    pre_local, rows, w_down = lax.optimization_barrier((pre_local, rows, w_down))
    pre_part = sum_y(pre_local)
    w_out = share(w_down[0].T)
    rows_next = swap_pair(rows, "c")
    (act_local,) = local(act_kernel, [((slots, units), BF)], rows, *w_out)
    act_local, rows_next = lax.optimization_barrier((act_local, rows_next))
    act_part = sum_y(act_local)

    pre_other = swap_pair(pre_part, "zh")
    copies = (8, slots // 8)
    (hidden,) = local(hidden_kernel, [(copies + (units,), BF)], pre_part, pre_other)
    hidden, act_part = lax.optimization_barrier((hidden, act_part))
    hidden = gather_y(hidden)
    act_other = swap_pair(act_part, "zh")
    (deltas,) = local(
        delta_kernel, [(copies + (2 * units,), BF)], pre_part, pre_other, act_part, act_other
    )
    deltas = gather_y(deltas)

    def to_next(value):
        sides = value.shape[1] // units
        cut = [
            value[:, side * units + step * hs :][:, :hs] for step in (1, 3) for side in range(sides)
        ]
        return swap_pair(jnp.concatenate(cut, axis=1), "c")

    shape = (width, hs)
    down_keep, down_away = local(
        down_kernel, [(shape, F32), (shape, BF)], rows, rows_next, hidden, to_next(hidden)
    )
    down_got = swap_pair(down_away, "zb")
    deltas, hidden, down_got = lax.optimization_barrier((deltas, hidden, down_got))
    (back,) = local(
        back_kernel, [((slots, 2 * width), BF)], hidden, deltas, *w_in, *w_out
    )
    back, ids, weight, deltas = lax.optimization_barrier((back, ids, weight, deltas))
    deltas_got = to_next(deltas)
    count = TOP * tok_rows
    place, column = local(
        place_kernel, [((slots, count), BF), ((count, count), F32)], ids, weight
    )
    back = swap(back.reshape(EXPERTS, CAP, 2 * width), OWN).reshape(slots, 2 * width)

    factor = 1.0 / math.sqrt(8 * tok_rows)

    def into(*refs):
        in_kernel(factor, *refs)

    shape = (width, 2 * hs)
    in_keep, in_away = local(
        into, [(shape, F32), (shape, BF)], rows, rows_next, deltas, deltas_got
    )
    gate_grad, up_grad = local(
        join_kernel, [((width, hs), F32)] * 2, in_keep, swap_pair(in_away, "zb")
    )
    down_grad = (down_keep + down_got.astype(F32)) * factor
    mixed, tokens_grad = local(home_kernel, [((tok_rows, width), F32)] * 2, place, column, back)
    return (mixed, tokens_grad, gate_grad[None], up_grad[None], down_grad.T[None])


def solution(mesh):
    fine = Mesh(mesh.devices.reshape(8, 2, 4, 4, 2, 2), GRP + EP)
    return jax.shard_map(
        body,
        mesh=fine,
        in_specs=(
            P(EP, GRP),
            P(EP, None),
            P(EP, None),
            P(EP, GRP),
            P(EP, GRP, None),
            P(EP, GRP, None),
            P(EP, None, GRP),
        ),
        out_specs=(
            P(EP, GRP),
            P(EP, GRP),
            P(EP, GRP, None),
            P(EP, GRP, None),
            P(EP, None, GRP),
        ),
        check_vma=False,
    )
```
